512 devices in a mesh: value: 64 (over x, z, core), replica: 8 (over y).
Axes of the slice: x: 4, y: 8, z: 8, core: 2. Of those that a mesh axis runs over, the one named last changes fastest.
Arguments:
- key_blocks: int32 [65536, 2], P(('value', 'replica')), may hold values from 0 to 63, all different within a row; in each aligned block of 128 rows (0 to 127, 128 to 255, ...) at most 5 rows name the same one
- key_rows: int32 [65536, 32], P(('value', 'replica')), may hold values from 0 to 127, as said below
- weights: float32 [65536, 32], P(('value', 'replica')), may hold values from 0.02 to 0.5
- value_table: bfloat16 [8192, 4096], P('value'), may hold values from -6 to 6
- cotangent: bfloat16 [65536, 4096], P(('value', 'replica')), may hold values from -0.75 to 0.75
Outputs:
- memory_out: bfloat16 [65536, 4096], P(('value', 'replica'))
- weight_grad: bfloat16 [65536, 32], P(('value', 'replica'))
- table_grad: bfloat16 [8192, 4096], P(('value', 'replica'))
The draws below stay inside these ranges and needn't reach their ends.
Inputs may be any that keep to these rules, and one draw needn't show every extreme that they name: `key_blocks`: in each row the 2 numbers differ; among the rows of one device (aligned blocks of 128 rows) no number appears more than 5 times, and some number appears exactly 5 times. `key_rows`: the 16 numbers of one key block (positions 16 g to 16 g + 15) differ.
All inputs are finite; a program needn't handle non-finite values.
Results may differ from the reference program's by a relative error of at most 0.017.
Values may be sent and summed in bfloat16 or wider, within the bound.
No kernel may reach another device: no remote copies, remote signals or barrier semaphores. Data moves between devices by JAX's collectives and lax.ppermute only.
A program may use at most 64 MiB of HBM per device.

```python
import math
import jax
import jax.numpy as jnp
import numpy as np
from jax import lax

D = 4096
ROWS_DEV = 128
GROUPS = 2
PICKS = 16
TOK_DEV = 128
TOPK = 32
OWNERS = 64
ROWS = 8192
CAP = 5
TOKENS = 65536
N_VALUE = 64
N_REPLICA = 8


def draw_key_rows(key, part):
    key = jax.random.fold_in(key, 7)
    leading_key_half, second_key = jax.random.split(key)
    begin_positions = jax.random.randint(leading_key_half, (TOKENS, GROUPS, 1), 0, ROWS_DEV)
    spaces = jax.random.randint(second_key, (TOKENS, GROUPS, PICKS - 1), 1, ROWS_DEV // PICKS + 1)
    index_shifts = jnp.concatenate([jnp.zeros((TOKENS, GROUPS, 1), jnp.int32), jnp.cumsum(spaces, axis=-1)], axis=-1)
    return ((begin_positions + index_shifts) % ROWS_DEV).reshape(TOKENS, GROUPS * PICKS).astype(jnp.int32)


def level_of(own_key, extent, cuts, low, high):
    loudness, own = 1.0, jax.random.fold_in(own_key, 6)
    for dim, shards_of in cuts:
        heights = jnp.exp(jax.random.uniform(jax.random.fold_in(own, dim), (shards_of,), jnp.float32, low / len(cuts), high / len(cuts)))
        loudness = loudness * jnp.repeat(heights, extent[dim] // shards_of).reshape([-1 if axis == dim else 1 for axis in range(len(extent))])
    return loudness


def routed_block(key, own, number, rows, count, top, limit, lean):
    ranking = jax.random.permutation(key, count)
    crowded, ordinary = portions_of(count, rows * top, limit, lean, True), portions_of(count, rows * top, limit, lean, False)
    places = jnp.arange(count)

    def named(tallies, rotation):
        used = int((tallies > 0).sum())
        fixed = max(1, used // 4)
        passed = fixed + (places - fixed + rotation * (used - fixed)) % max(1, count - fixed)
        return jnp.zeros((count,), jnp.int32).at[ranking[jnp.where(places < fixed, places, passed)]].set(jnp.asarray(tallies, jnp.int32))

    tallies = jnp.where(number % 4 == 0, named(crowded, number // 4), named(ordinary, number - number // 4 - 1))
    mixed = jax.random.permutation(jax.random.fold_in(own, 3), count)
    source_of, sink = mixed[0:count // 2 * 2:2], mixed[1:count // 2 * 2:2]
    slack = jnp.minimum(tallies[source_of] - 1, limit - tallies[sink]) // 2
    slack = jnp.where((source_of == ranking[0]) | (sink == ranking[0]) | (tallies[sink] == 0), 0, jnp.maximum(slack, 0))
    passed = jax.random.randint(jax.random.fold_in(own, 4), (count // 2,), 0, 1 << 20) % (slack + 1)
    tallies = tallies.at[source_of].add(-passed).at[sink].add(passed)
    labels = jnp.searchsorted(jnp.cumsum(tallies), jnp.arange(rows * top), side="right").astype(jnp.int32)
    listing = labels.reshape(top, rows).T
    listing = listing[jax.random.permutation(jax.random.fold_in(own, 1), rows)]
    rotation = jax.random.randint(jax.random.fold_in(own, 2), (rows, 1), 0, top)
    return jnp.take_along_axis(listing, (jnp.arange(top)[None, :] + rotation) % top, axis=1)


def portions_of(count, total, reach, skew, full):
    loads = [(1 << 20) // math.isqrt(standing ** skew) + 1 for standing in range(1, count + 1)]
    largest = reach if full else min(reach, max(-(-total // count), total * loads[0] // sum(loads)))
    least = 1 if total - largest >= count - 1 else 0
    counts, surplus = [largest] + [least] * (count - 1), total - largest - least * (count - 1)
    while surplus > 0:
        free = [i for i in range(1, count) if counts[i] < largest] or [i for i in range(1, count) if counts[i] < reach]
        pool, budget = sum([loads[i] for i in free]), surplus
        for i in free:
            extra = min(reach - counts[i], max(1, budget * loads[i] // pool), surplus)
            counts[i] = counts[i] + extra
            surplus = surplus - extra
    return np.array(counts)


def gaussian(rng, dims, width, reach, cuts=(), dtype=jnp.bfloat16):
    entries = width * jax.random.normal(rng, dims, jnp.float32)
    if cuts:
        entries = entries * level_of(rng, dims, cuts, -0.22, 0.18)
    return jnp.clip(entries, -reach, reach).astype(dtype)


def setup_inputs(seed: int = 0) -> dict:
    arg_keys = jax.random.split(jax.random.key(seed), 6)
    key_blocks_keys = jax.random.split(jax.random.fold_in(arg_keys[0], 1), TOKENS // TOK_DEV)
    key_blocks_turns = jax.random.permutation(jax.random.fold_in(arg_keys[0], 3), TOKENS // TOK_DEV)
    key_blocks = jax.vmap(lambda own, number: routed_block(jax.random.fold_in(arg_keys[0], 2), own, number, TOK_DEV, OWNERS, GROUPS, CAP, 2))(key_blocks_keys, key_blocks_turns).reshape((TOKENS, GROUPS))
    key_rows = draw_key_rows(jax.random.fold_in(arg_keys[5], 71), 0)
    weights = jnp.clip(jnp.exp(math.log(0.5) - 3.218876 * jax.random.uniform(arg_keys[2], (TOKENS, TOPK), jnp.float32) ** level_of(arg_keys[2], (TOKENS, TOPK), ((0, 512),), -0.2, 0.2)), 0.02, 0.5)
    value_table = gaussian(arg_keys[3], (ROWS, D), 1.0, 6.0, ((0, 64),))
    cotangent = gaussian(arg_keys[4], (TOKENS, D), 0.125, 0.75, ((0, 512),))
    return {"key_blocks": key_blocks, "key_rows": key_rows, "weights": weights, "value_table": value_table, "cotangent": cotangent}


def reference(key_blocks, key_rows, weights, value_table, cotangent):
    index = (jnp.repeat(key_blocks, PICKS, axis=1) * ROWS_DEV + key_rows).astype(jnp.int32)
    rounded_weights = lax.optimization_barrier(weights.astype(jnp.bfloat16)).astype(jnp.float32)
    count_of_blocks = TOKENS // TOK_DEV

    def forward(pieces):
        block_index, block_weights, gradient_per_block = pieces
        collected_values = value_table[block_index].astype(jnp.float32)
        terms = (block_weights[:, :, None] * collected_values).reshape(TOK_DEV, GROUPS, PICKS, D)
        partial_value = lax.optimization_barrier(jnp.sum(terms, axis=2).astype(jnp.bfloat16)).astype(jnp.float32)
        output = jnp.sum(partial_value, axis=1).astype(jnp.bfloat16)
        gradient_rows = jnp.einsum("fq,frq->fr", gradient_per_block.astype(jnp.float32), collected_values).astype(jnp.bfloat16)
        return output, gradient_rows

    memory_out, weight_grad = lax.map(forward, (index.reshape(count_of_blocks, TOK_DEV, TOPK),
                                                rounded_weights.reshape(count_of_blocks, TOK_DEV, TOPK),
                                                cotangent.reshape(count_of_blocks, TOK_DEV, D)))
    memory_out = memory_out.reshape(TOKENS, D)
    weight_grad = weight_grad.reshape(TOKENS, TOPK)

    index_split = jnp.swapaxes(index.reshape(N_VALUE, N_REPLICA, TOK_DEV, TOPK), 0, 1)
    weight_split = jnp.swapaxes(rounded_weights.reshape(N_VALUE, N_REPLICA, TOK_DEV, TOPK), 0, 1)
    grad_split = jnp.swapaxes(cotangent.reshape(N_VALUE, N_REPLICA, TOK_DEV, D), 0, 1)

    def per_replica(total, pieces):
        replica_index, replica_weights, replica_grads = pieces

        def add_block(accum, block):
            block_index, block_weights, gradient_per_block = block
            update = block_weights[:, :, None] * gradient_per_block.astype(jnp.float32)[:, None, :]
            return accum.at[block_index.reshape(-1)].add(update.reshape(-1, D)), None

        accum, _ = lax.scan(add_block, jnp.zeros((ROWS, D), jnp.float32),
                            (replica_index, replica_weights, replica_grads))
        rounded_rows = lax.optimization_barrier(accum.astype(jnp.bfloat16)).astype(jnp.float32)
        return total + rounded_rows, None

    total, _ = lax.scan(per_replica, jnp.zeros((ROWS, D), jnp.float32), (index_split, weight_split, grad_split))
    return memory_out, weight_grad, total.astype(jnp.bfloat16)
```

```python
import functools

import jax
import jax.numpy as jnp
import numpy as np
from jax import lax
from jax.experimental import pallas as pl
from jax.experimental.pallas import tpu as pltpu
from jax.sharding import Mesh
from jax.sharding import PartitionSpec as P

CAP = 5
CHIPS = 32
GROUP_SLOTS = 512
TAGS = 384
BF16 = jnp.bfloat16
F32 = jnp.float32
VMEM_LIMIT = 56 * 1024 * 1024


def iota(shape, dim):
    return lax.broadcasted_iota(jnp.int32, shape, dim)


def contract(a, b, da, db):
    return lax.dot_general(a, b, (((da,), (db,)), ((), ())), preferred_element_type=F32)


def spread_table():
    m = np.zeros((TAGS, 2 * GROUP_SLOTS), np.float32)
    for lane in range(2 * CHIPS * CAP):
        core, rest = divmod(lane, CHIPS * CAP)
        m[lane, rest // CAP * 16 + core * 8 + rest % CAP] = 1
    for i in range(2 * CAP):
        m[2 * CHIPS * CAP + i, GROUP_SLOTS + i // CAP * 8 + i % CAP :: 16] = 1
    return m


def tag_kernel(place_ref, blocks_ref, rows_ref, weights_ref, own_ref, other_ref):
    core = place_ref[0]
    n = 256
    owner = jnp.concatenate([blocks_ref[:, 0:1], blocks_ref[:, 1:2]], axis=0)
    hot = (owner == iota((n, 64), 1)).astype(F32)
    lower = (iota((n, n), 1) < iota((n, n), 0)).astype(BF16)
    before = contract(lower, hot.astype(BF16), 1, 0)
    rank = jnp.sum(before * hot, axis=1, keepdims=True).astype(jnp.int32)
    half = owner & 1
    chip = owner >> 1
    rows = rows_ref[...].astype(F32).astype(BF16)
    rows = jnp.concatenate([rows[:, :16], rows[:, 16:]], axis=0)
    weights = weights_ref[...].astype(BF16)
    weights = jnp.concatenate([weights[:, :16], weights[:, 16:]], axis=0)
    entry = iota((n, CHIPS), 0) + 1
    lanes = iota((n, TAGS), 1)
    token_place = (lanes == 2 * CHIPS * CAP + core * CAP + rank).astype(F32).astype(BF16)
    for out, mine in ((own_ref, core), (other_ref, 1 - core)):
        slot = jnp.where(half == mine, core * (CHIPS * CAP) + chip * CAP + rank, -1)
        hits = (lanes == slot).astype(F32).astype(BF16)
        tokens = jnp.where(jnp.where(half == mine, chip, -1) == iota((n, CHIPS), 1), entry, 0)
        tokens = tokens.astype(F32).astype(BF16)
        tags = jnp.concatenate([contract(rows, hits, 0, 0), contract(weights, hits, 0, 0)], axis=0)
        tags = (tags + contract(tokens, token_place, 0, 0)).astype(BF16)
        for i in range(3):
            out[i] = tags[:, 128 * i : 128 * (i + 1)]


def mix_kernel(place_ref, spread_ref, got_ref, mix_ref, pick_ref, token_ref, tags_ref, wide_ref):
    core = place_ref[0]
    flip = place_ref[1] * 16
    for g in range(CHIPS):
        for i in range(3):
            tags_ref[g * 32 : (g + 1) * 32, 128 * i : 128 * (i + 1)] = got_ref[g, 32 * i : 32 * (i + 1), :]
    for i in range(4):
        cols = slice(256 * i, 256 * (i + 1))
        wide_ref[:, cols] = contract(tags_ref[...], spread_ref[:, cols], 1, 0)
    shard_of = iota((CHIPS, GROUP_SLOTS), 1) // 16 == iota((CHIPS, GROUP_SLOTS), 0)
    second = (iota((1, GROUP_SLOTS), 1) & 8) != 0
    far = jnp.where(second, 1 - core, core).astype(F32)
    position = iota((128, GROUP_SLOTS), 0).astype(F32).astype(BF16)

    def group(g, _):
        at = pl.multiple_of(g * 32, 32)
        rows = wide_ref[pl.ds(at, 16), 0:GROUP_SLOTS]
        weights = wide_ref[pl.ds(at + 16, 16), 0:GROUP_SLOTS].astype(BF16)
        tokens = wide_ref[pl.ds(at, 32), GROUP_SLOTS : 2 * GROUP_SLOTS]
        tag = jnp.sum(jnp.where(shard_of, tokens, 0.0), axis=0, keepdims=True)
        valid = tag > 0.5
        second_block = (tag > 128.5).astype(F32)
        token = tag - 1.0 - 128.0 * second_block
        quarter = (
            (token > 31.5).astype(F32) + (token > 63.5).astype(F32) + (token > 95.5).astype(F32)
        )
        full_place = jnp.where(valid, far * 128.0 + token, -1.0)
        fold_place = jnp.where(valid, far * 32.0 + token - 32.0 * quarter, -1.0)
        part = jnp.where(valid, quarter * 2.0 + second_block, -1.0)
        token_ref[g, 0:1, :] = full_place
        token_ref[g, 1:2, :] = fold_place
        rows = (rows.astype(jnp.int32) ^ flip).astype(F32)
        picks = jnp.concatenate([jnp.where(part == float(i), rows, -1.0) for i in range(8)], axis=0)
        picks = picks.astype(BF16)
        rows = rows.astype(BF16)
        mix = jnp.zeros((128, GROUP_SLOTS), BF16)
        for k in range(16):
            mix = jnp.where(rows[k : k + 1, :] == position, weights[k : k + 1, :], mix)
        here = pl.ds(pl.multiple_of(g * 16, 16), 16)
        mix_ref[:, here, :] = mix.T.reshape(CHIPS, 16, 128)
        pick_ref[:, here, :] = picks.T.reshape(CHIPS, 16, 128)
        return 0

    lax.fori_loop(0, CHIPS, group, 0)


def value_kernel(mix_ref, token_ref, table_ref, out_ref, sums_ref):
    def shard(o, _):
        table = table_ref[:, o].reshape(128, 128)
        sums_ref[o] = contract(mix_ref[o], table, 1, 0).astype(BF16)
        return 0

    lax.fori_loop(0, CHIPS, shard, 0)
    token_rows = iota((256, GROUP_SLOTS), 0).astype(F32).astype(BF16)

    def group(g, _):
        sums = sums_ref[:, pl.ds(pl.multiple_of(g * 16, 16), 16), :].reshape(GROUP_SLOTS, 128)
        place = token_ref[g, 0:1, :].astype(BF16)
        hits = jnp.where(place == token_rows, jnp.ones((), BF16), jnp.zeros((), BF16))
        out = contract(hits, sums, 1, 0).astype(BF16)
        out_ref[0, g] = out[:128]
        out_ref[1, g] = out[128:]
        return 0

    lax.fori_loop(0, CHIPS, group, 0)


def grad_kernel(
    mix_ref, pick_ref, token_ref, table_ref, near_ref, far_ref, table_grad_ref, weight_ref, rows_ref
):
    token_rows = iota((256, GROUP_SLOTS), 0).astype(F32).astype(BF16)
    fold_rows = iota((64, GROUP_SLOTS), 0).astype(F32).astype(BF16)

    def gather(g, _):
        place = token_ref[g, 0:1, :].astype(BF16)
        hits = jnp.where(place == token_rows, jnp.ones((), BF16), jnp.zeros((), BF16))
        grads = jnp.concatenate([near_ref[g], far_ref[g]], axis=0)
        rows = contract(hits, grads, 0, 0).astype(BF16)
        rows_ref[:, pl.ds(pl.multiple_of(g * 16, 16), 16), :] = rows.reshape(CHIPS, 16, 128)
        return 0

    lax.fori_loop(0, CHIPS, gather, 0)

    def shard(o, _):
        rows = rows_ref[o]
        table_grad = contract(mix_ref[o], rows, 0, 0).astype(BF16)
        table_grad_ref[:, o] = table_grad.reshape(8, 16, 128)
        scores = contract(rows, table_ref[:, o].reshape(128, 128), 1, 1)
        picks = pick_ref[o].astype(F32).astype(jnp.int32)
        found = jnp.take_along_axis(
            scores, jnp.maximum(picks, 0), axis=1, mode="promise_in_bounds"
        )
        rows_ref[o] = jnp.where(picks >= 0, found, 0.0).astype(BF16)
        return 0

    lax.fori_loop(0, CHIPS, shard, 0)

    def group(g, _):
        found = rows_ref[:, pl.ds(pl.multiple_of(g * 16, 16), 16), :].reshape(GROUP_SLOTS, 128)
        place = token_ref[g, 1:2, :].astype(BF16)
        hits = jnp.where(place == fold_rows, jnp.ones((), BF16), jnp.zeros((), BF16))
        out = contract(hits, found, 1, 0).astype(BF16)
        weight_ref[0, g] = out[:32]
        weight_ref[1, g] = out[32:]
        return 0

    lax.fori_loop(0, CHIPS, group, 0)


def finish_kernel(got_ref, weight_ref, table_ref):
    def add(j, total):
        return total + got_ref[j, 0:32, :].astype(F32)

    total = lax.fori_loop(0, CHIPS, add, jnp.zeros((32, 128), F32))
    for i in range(4):
        weight_ref[32 * i : 32 * (i + 1), :] = total[:, 32 * i : 32 * (i + 1)].astype(BF16)
    for j in range(CHIPS):
        table_ref[:, 128 * j : 128 * (j + 1)] = got_ref[j, 32:48, :]


def call(kernel, out_shapes, *operands, scalars=0, scratch=(), cost=(0, 0)):
    vmem = pl.BlockSpec(memory_space=pltpu.VMEM)
    smem = pl.BlockSpec(memory_space=pltpu.SMEM)
    outs = tuple(jax.ShapeDtypeStruct(s, d) for s, d in out_shapes)
    return pl.pallas_call(
        kernel,
        out_shape=outs,
        in_specs=[smem] * scalars + [vmem] * (len(operands) - scalars),
        out_specs=tuple(vmem for _ in outs),
        scratch_shapes=[pltpu.VMEM(s, d) for s, d in scratch],
        compiler_params=pltpu.CompilerParams(vmem_limit_bytes=VMEM_LIMIT),
        cost_estimate=pl.CostEstimate(flops=cost[0], bytes_accessed=cost[1], transcendentals=0),
    )(*operands)


def swap_cores(v):
    return lax.ppermute(v, "core", [(0, 1), (1, 0)])


def across(v, bit):
    return lax.ppermute(v, "y", [(i, i ^ bit) for i in range(8)])


def exchange(v):
    return lax.all_to_all(v, ("x", "z"), split_axis=0, concat_axis=0, tiled=True)


def on_device(key_blocks, key_rows, weights, value_table, cotangent):
    core = lax.axis_index("core")
    y = lax.axis_index("y")
    place = jnp.stack([core, y]).astype(jnp.int32)

    own, other = call(
        tag_kernel,
        [((3, 32, 128), BF16)] * 2,
        place,
        key_blocks,
        key_rows,
        weights,
        scalars=1,
    )
    tags = (own + swap_cores(other)).reshape(1, 96, 128)
    table_part = lax.dynamic_slice_in_dim(value_table, y * 16, 16, axis=0)
    table_part = jnp.transpose(table_part.reshape(16, CHIPS, 128), (1, 0, 2))
    first = jnp.concatenate([jnp.broadcast_to(tags, (CHIPS, 96, 128)), table_part], axis=1)
    got_first = exchange(first)

    grads = jnp.transpose(cotangent.reshape(128, CHIPS, 128), (1, 0, 2))
    near_grads = exchange(lax.optimization_barrier((grads, got_first))[0])

    mix, picks, tokens = call(
        mix_kernel,
        [((CHIPS, GROUP_SLOTS, 128), BF16)] * 2 + [((CHIPS, 8, GROUP_SLOTS), F32)],
        place,
        jnp.asarray(spread_table(), BF16),
        got_first,
        scalars=1,
        scratch=[((CHIPS * 32, TAGS), BF16), ((CHIPS * 32, 2 * GROUP_SLOTS), F32)],
        cost=(10**9, 10 * 2**20),
    )
    table = got_first[:, 96:, :].reshape(1, CHIPS, 16, 128)
    for bit in (1, 2, 4):
        table = jnp.concatenate([table, across(table, bit)], axis=0)
    (sums,) = call(
        value_kernel,
        [((2, CHIPS, 128, 128), BF16)],
        mix,
        tokens,
        table,
        scratch=[((CHIPS, GROUP_SLOTS, 128), BF16)],
        cost=(2 * 10**9, 8 * 2**20),
    )
    out = (sums[0].astype(F32) + swap_cores(sums[1]).astype(F32)).astype(BF16)
    got_out = exchange(lax.optimization_barrier((out, near_grads))[0])

    far_grads = swap_cores(near_grads)
    table_grad, weight_grad = call(
        grad_kernel,
        [((8, CHIPS, 16, 128), BF16), ((2, CHIPS, 32, 128), BF16)],
        mix,
        picks,
        tokens,
        table,
        near_grads,
        far_grads,
        scratch=[((CHIPS, GROUP_SLOTS, 128), BF16)],
        cost=(2 * 10**9, 12 * 2**20),
    )
    for count in (4, 2, 1):
        received = across(table_grad[count:], count)
        table_grad = (table_grad[:count].astype(F32) + received.astype(F32)).astype(BF16)
    weight_grad = (
        weight_grad[0].astype(F32) + swap_cores(weight_grad[1]).astype(F32)
    ).astype(BF16)
    last = jnp.concatenate([weight_grad, table_grad[0]], axis=1)
    got_last = exchange(lax.optimization_barrier((last, got_out))[0])
    memory_out = jnp.transpose(got_out, (1, 0, 2)).reshape(128, 4096)
    weight_out, table_out = call(
        finish_kernel, [((128, 32), BF16), ((16, 4096), BF16)], got_last
    )
    return memory_out, weight_out, table_out


def solution(mesh):
    fine = Mesh(mesh.devices.reshape(4, 8, 2, 8), ("x", "z", "core", "y"))
    tokens = P(("x", "z", "core", "y"), None)
    return jax.shard_map(
        on_device,
        mesh=fine,
        in_specs=(tokens, tokens, tokens, P(("x", "z", "core"), None), tokens),
        out_specs=(tokens, tokens, tokens),
        check_vma=False,
    )
```

```python
import jax
import jax.numpy as jnp
import numpy as np
from jax import lax
from jax.experimental import pallas as pl
from jax.experimental.pallas import tpu as pltpu
from jax.sharding import Mesh
from jax.sharding import PartitionSpec as P

CAP = 5
CHIPS = 32
GROUP_SLOTS = 512
TAGS = 384
BF16 = jnp.bfloat16
F32 = jnp.float32


def iota(shape, dim):
    return lax.broadcasted_iota(jnp.int32, shape, dim)


def contract(a, b, da, db):
    return lax.dot_general(a, b, (((da,), (db,)), ((), ())), preferred_element_type=F32)


def spread_table():
    m = np.zeros((TAGS, 2 * GROUP_SLOTS), np.float32)
    for lane in range(2 * CHIPS * CAP):
        core, rest = divmod(lane, CHIPS * CAP)
        m[lane, rest // CAP * 16 + core * 8 + rest % CAP] = 1
    for i in range(2 * CAP):
        m[2 * CHIPS * CAP + i, GROUP_SLOTS + i // CAP * 8 + i % CAP :: 16] = 1
    return m


def tag_kernel(blocks_ref, rows_ref, weights_ref, own_ref, other_ref):
    core = lax.axis_index("core")
    n = 256
    owner = jnp.concatenate([blocks_ref[0:1, :], blocks_ref[1:2, :]], axis=1)
    hot = (owner == iota((64, n), 0)).astype(F32)
    upper = (iota((n, n), 0) < iota((n, n), 1)).astype(BF16)
    before = contract(hot.astype(BF16), upper, 1, 0)
    rank = jnp.sum(before * hot, axis=0, keepdims=True).astype(jnp.int32)
    half = owner & 1
    chip = owner >> 1
    rows = rows_ref[...].astype(F32).astype(BF16)
    rows = jnp.concatenate([rows[:16], rows[16:]], axis=1)
    weights = weights_ref[...].astype(BF16)
    weights = jnp.concatenate([weights[:16], weights[16:]], axis=1)
    entry = iota((CHIPS, n), 1) + 1
    lanes = iota((TAGS, n), 0)
    token_place = (lanes == 2 * CHIPS * CAP + core * CAP + rank).astype(F32).astype(BF16)
    for out, mine in ((own_ref, core), (other_ref, 1 - core)):
        slot = jnp.where(half == mine, core * (CHIPS * CAP) + chip * CAP + rank, -1)
        hits = (lanes == slot).astype(F32).astype(BF16)
        tokens = jnp.where(jnp.where(half == mine, chip, -1) == iota((CHIPS, n), 0), entry, 0)
        tokens = tokens.astype(F32).astype(BF16)
        tags = jnp.concatenate([contract(rows, hits, 1, 1), contract(weights, hits, 1, 1)], axis=0)
        tags = (tags + contract(tokens, token_place, 1, 1)).astype(BF16)
        for i in range(3):
            out[i] = tags[:, 128 * i : 128 * (i + 1)]


def split_kernel(grads_ref, out_ref):
    for j in range(CHIPS):
        out_ref[j] = grads_ref[:, 128 * j : 128 * (j + 1)]


def first_kernel(own_ref, other_ref, table_ref, out_ref):
    y = lax.axis_index("y")
    tags = own_ref[...].reshape(96, 128) + other_ref[...].reshape(96, 128)
    for j in range(CHIPS):
        out_ref[j, 0:96, :] = tags
    for i in range(4):
        block = (((y >> 1) ^ i) << 1) | (y & 1)
        rows = pl.ds(pl.multiple_of(block * 16, 16), 16)
        for j in range(CHIPS):
            out_ref[j, 96 + 16 * i : 112 + 16 * i, :] = table_ref[rows, 128 * j : 128 * (j + 1)]


def mix_kernel(spread_ref, got_ref, mix_ref, pick_ref, token_ref, tags_ref, wide_ref):
    core = lax.axis_index("core")
    flip = lax.axis_index("y") * 16
    for g in range(CHIPS):
        for i in range(3):
            tags_ref[g * 32 : (g + 1) * 32, 128 * i : 128 * (i + 1)] = got_ref[g, 32 * i : 32 * (i + 1), :]
    for i in range(4):
        cols = slice(256 * i, 256 * (i + 1))
        wide_ref[:, cols] = contract(tags_ref[...], spread_ref[:, cols], 1, 0)
    shard_of = iota((CHIPS, GROUP_SLOTS), 1) // 16 == iota((CHIPS, GROUP_SLOTS), 0)
    second = (iota((1, GROUP_SLOTS), 1) & 8) != 0
    far = jnp.where(second, 1 - core, core).astype(F32)
    position = iota((128, GROUP_SLOTS), 0).astype(F32).astype(BF16)

    def group(g, _):
        at = pl.multiple_of(g * 32, 32)
        rows = wide_ref[pl.ds(at, 16), 0:GROUP_SLOTS]
        weights = wide_ref[pl.ds(at + 16, 16), 0:GROUP_SLOTS].astype(BF16)
        tokens = wide_ref[pl.ds(at, 32), GROUP_SLOTS : 2 * GROUP_SLOTS]
        tag = jnp.sum(jnp.where(shard_of, tokens, 0.0), axis=0, keepdims=True)
        valid = tag > 0.5
        second_block = (tag > 128.5).astype(F32)
        token = tag - 1.0 - 128.0 * second_block
        quarter = (
            (token > 31.5).astype(F32) + (token > 63.5).astype(F32) + (token > 95.5).astype(F32)
        )
        full_place = jnp.where(valid, far * 128.0 + token, -1.0)
        fold_place = jnp.where(valid, far * 32.0 + token - 32.0 * quarter, -1.0)
        part = jnp.where(valid, quarter * 2.0 + second_block, -1.0)
        token_ref[g, 0:1, :] = full_place
        token_ref[g, 1:2, :] = fold_place
        rows = (rows.astype(jnp.int32) ^ flip).astype(F32)
        picks = jnp.concatenate([jnp.where(part == float(i), rows, -1.0) for i in range(8)], axis=0)
        picks = picks.astype(BF16)
        rows = rows.astype(BF16)
        mix = jnp.zeros((128, GROUP_SLOTS), BF16)
        for k in range(16):
            mix = jnp.where(rows[k : k + 1, :] == position, weights[k : k + 1, :], mix)
        here = pl.ds(pl.multiple_of(g * 16, 16), 16)
        mix_ref[:, here, :] = mix.T.reshape(CHIPS, 16, 128)
        pick_ref[:, here, :] = picks.T.reshape(CHIPS, 16, 128)
        return 0

    lax.fori_loop(0, CHIPS, group, 0, unroll=4)


def table_of(got_ref, table_ref, o):
    pieces = []
    for i in range(4):
        pieces += [got_ref[o, 96 + 16 * i : 112 + 16 * i, :], table_ref[o, 16 * i : 16 * (i + 1), :]]
    return jnp.concatenate(pieces, axis=0)


def value_kernel(mix_ref, token_ref, got_ref, table_ref, near_ref, far_ref, sums_ref):
    def shard(o, _):
        sums_ref[o] = contract(mix_ref[o], table_of(got_ref, table_ref, o), 1, 0).astype(BF16)
        return 0

    lax.fori_loop(0, CHIPS, shard, 0, unroll=8)
    token_rows = iota((256, GROUP_SLOTS), 0).astype(F32).astype(BF16)

    def group(g, _):
        sums = sums_ref[:, pl.ds(pl.multiple_of(g * 16, 16), 16), :].reshape(GROUP_SLOTS, 128)
        place = token_ref[g, 0:1, :].astype(BF16)
        hits = jnp.where(place == token_rows, jnp.ones((), BF16), jnp.zeros((), BF16))
        out = contract(hits, sums, 1, 0).astype(BF16)
        near_ref[g] = out[:128]
        far_ref[g] = out[128:]
        return 0

    lax.fori_loop(0, CHIPS, group, 0, unroll=8)


def table_grad_kernel(mix_ref, token_ref, near_ref, far_ref, rows_ref, *grad_refs):
    token_rows = iota((256, GROUP_SLOTS), 0).astype(F32).astype(BF16)

    def gather(g, _):
        place = token_ref[g, 0:1, :].astype(BF16)
        hits = jnp.where(place == token_rows, jnp.ones((), BF16), jnp.zeros((), BF16))
        grads = jnp.concatenate([near_ref[g], far_ref[g]], axis=0)
        rows = contract(hits, grads, 0, 0).astype(BF16)
        rows_ref[:, pl.ds(pl.multiple_of(g * 16, 16), 16), :] = rows.reshape(CHIPS, 16, 128)
        return 0

    lax.fori_loop(0, CHIPS, gather, 0, unroll=8)

    def shard(o, _):
        grad = contract(mix_ref[o], rows_ref[o], 0, 0).astype(BF16)
        for m in range(8):
            grad_refs[m][o] = grad[16 * m : 16 * (m + 1)]
        return 0

    lax.fori_loop(0, CHIPS, shard, 0, unroll=8)


def weight_grad_kernel(rows_ref, pick_ref, token_ref, got_ref, table_ref, near_ref, far_ref, found_ref):
    fold_rows = iota((64, GROUP_SLOTS), 0).astype(F32).astype(BF16)

    def shard(o, _):
        scores = contract(rows_ref[o], table_of(got_ref, table_ref, o), 1, 1)
        picks = pick_ref[o].astype(F32).astype(jnp.int32)
        found = jnp.take_along_axis(scores, jnp.maximum(picks, 0), axis=1, mode="promise_in_bounds")
        found_ref[o] = jnp.where(picks >= 0, found, 0.0).astype(BF16)
        return 0

    lax.fori_loop(0, CHIPS, shard, 0, unroll=8)

    def group(g, _):
        found = found_ref[:, pl.ds(pl.multiple_of(g * 16, 16), 16), :].reshape(GROUP_SLOTS, 128)
        place = token_ref[g, 1:2, :].astype(BF16)
        hits = jnp.where(place == fold_rows, jnp.ones((), BF16), jnp.zeros((), BF16))
        out = contract(hits, found, 1, 0).astype(BF16)
        near_ref[g] = out[:32]
        far_ref[g] = out[32:]
        return 0

    lax.fori_loop(0, CHIPS, group, 0, unroll=8)


def last_kernel(near_ref, far_ref, *refs):
    out_ref = refs[-1]

    def chip(j, _):
        out_ref[j, 0:32, :] = (near_ref[j].astype(F32) + far_ref[j].astype(F32)).astype(BF16)
        total = refs[0][j].astype(F32)
        for ref in refs[1:-1]:
            total += ref[j].astype(F32)
        out_ref[j, 32:48, :] = total.astype(BF16)
        return 0

    lax.fori_loop(0, CHIPS, chip, 0, unroll=4)


def finish_kernel(got_ref, weight_ref, table_ref):
    def add(j, total):
        return total + got_ref[j, 0:32, :].astype(F32)

    total = lax.fori_loop(0, CHIPS, add, jnp.zeros((32, 128), F32), unroll=8)
    total = jnp.concatenate([total[:, 32 * i : 32 * (i + 1)] for i in range(4)], axis=0)
    weight_ref[...] = total.T.astype(BF16)
    for j in range(CHIPS):
        table_ref[:, 128 * j : 128 * (j + 1)] = got_ref[j, 32:48, :]


def call(kernel, out_shapes, *operands, scratch=(), cost=(0, 0), limit=16):
    vmem = pl.BlockSpec(memory_space=pltpu.VMEM)
    outs = tuple(jax.ShapeDtypeStruct(s, BF16) if not isinstance(s, jax.ShapeDtypeStruct) else s for s in out_shapes)
    return pl.pallas_call(
        kernel,
        out_shape=outs,
        in_specs=[vmem] * len(operands),
        out_specs=tuple(vmem for _ in outs),
        scratch_shapes=[pltpu.VMEM(s, d) for s, d in scratch],
        compiler_params=pltpu.CompilerParams(vmem_limit_bytes=limit * 2**20),
        cost_estimate=pl.CostEstimate(flops=cost[0], bytes_accessed=cost[1], transcendentals=0),
    )(*operands)


def swap_cores(v):
    return lax.ppermute(v, "core", [(0, 1), (1, 0)])


def across(v, bits):
    return lax.ppermute(v, "y", [(i, i ^ bits) for i in range(8)])


def exchange(v):
    return lax.all_to_all(v, ("x", "z"), split_axis=0, concat_axis=0, tiled=True)


def after(v, *others):
    return lax.optimization_barrier((v, *others))[0]


def on_device(key_blocks, key_rows, weights, value_table, cotangent):
    own, other = call(
        tag_kernel, [(3, 32, 128)] * 2, key_blocks.T, key_rows.T, weights.T, cost=(10**8, 2**20)
    )
    other = swap_cores(other)
    (grads,) = call(split_kernel, [(CHIPS, 128, 128)], cotangent, cost=(0, 2 * 2**20))
    other, grads = lax.optimization_barrier((other, grads))
    (first,) = call(first_kernel, [(CHIPS, 160, 128)], own, other, value_table, cost=(0, 3 * 2**20))
    got_first = exchange(first)
    near_grads = exchange(after(grads, got_first))

    table = across(got_first[:, 96:, :], 1)
    mix, picks, tokens = call(
        mix_kernel,
        [(CHIPS, GROUP_SLOTS, 128)] * 2 + [jax.ShapeDtypeStruct((CHIPS, 8, GROUP_SLOTS), F32)],
        jnp.asarray(spread_table(), BF16),
        got_first,
        scratch=[((CHIPS * 32, TAGS), BF16), ((CHIPS * 32, 2 * GROUP_SLOTS), F32)],
        cost=(10**9, 10 * 2**20),
        limit=24,
    )
    near, far = call(
        value_kernel,
        [(CHIPS, 128, 128)] * 2,
        mix,
        tokens,
        got_first,
        table,
        scratch=[((CHIPS, GROUP_SLOTS, 128), BF16)],
        cost=(2 * 10**9, 8 * 2**20),
    )
    out = (near.astype(F32) + swap_cores(far).astype(F32)).astype(BF16)
    got_out = exchange(after(out, near_grads))

    far_grads = swap_cores(near_grads)
    rows, *table_grads = call(
        table_grad_kernel,
        [(CHIPS, GROUP_SLOTS, 128)] + [(CHIPS, 16, 128)] * 8,
        mix,
        tokens,
        near_grads,
        far_grads,
        cost=(2 * 10**9, 12 * 2**20),
    )
    table_grads = [table_grads[0]] + [across(table_grads[m], m) for m in range(1, 8)]
    near, far = call(
        weight_grad_kernel,
        [(CHIPS, 32, 128)] * 2,
        rows,
        picks,
        tokens,
        got_first,
        table,
        scratch=[((CHIPS, GROUP_SLOTS, 128), BF16)],
        cost=(2 * 10**9, 12 * 2**20),
    )
    (last,) = call(
        last_kernel, [(CHIPS, 48, 128)], near, swap_cores(far), *table_grads, cost=(0, 2 * 2**20)
    )
    got_last = exchange(after(last, got_out))
    memory_out = jnp.transpose(got_out, (1, 0, 2)).reshape(128, 4096)
    weight_out, table_out = call(finish_kernel, [(32, 128), (16, 4096)], got_last)
    return memory_out, weight_out.T, table_out


def solution(mesh):
    fine = Mesh(mesh.devices.reshape(4, 8, 2, 8), ("x", "z", "core", "y"))
    tokens = P(("x", "z", "core", "y"), None)
    return jax.shard_map(
        on_device,
        mesh=fine,
        in_specs=(tokens, tokens, tokens, P(("x", "z", "core"), None), tokens),
        out_specs=(tokens, tokens, tokens),
        check_vma=False,
    )
```

```python
import jax
import jax.numpy as jnp
from jax import lax
from jax.experimental import pallas as pl
from jax.experimental.pallas import tpu as pltpu
from jax.sharding import Mesh
from jax.sharding import PartitionSpec as P

CAP = 5
CHIPS = 32
GROUP_SLOTS = 512
TAGS = 384
BF16 = jnp.bfloat16
F32 = jnp.float32


def iota(shape, dim):
    return lax.broadcasted_iota(jnp.int32, shape, dim)


def contract(a, b, da, db):
    return lax.dot_general(a, b, (((da,), (db,)), ((), ())), preferred_element_type=F32)


def prepare_kernel(
    blocks_any,
    rows_any,
    weights_any,
    table_any,
    grads_any,
    own_ref,
    other_ref,
    half_ref,
    out_ref,
    blocks_ref,
    rows_ref,
    weights_ref,
    table_ref,
    grads_ref,
    sems,
):
    anys = (blocks_any, rows_any, weights_any, grads_any, table_any)
    refs = (blocks_ref, rows_ref, weights_ref, grads_ref, table_ref)
    copies = [pltpu.make_async_copy(a, r, sems.at[i]) for i, (a, r) in enumerate(zip(anys, refs))]
    for copy in copies:
        copy.start()
    for copy in copies[:3]:
        copy.wait()
    tags(blocks_ref, rows_ref, weights_ref, own_ref, other_ref)
    copies[3].wait()
    for j in range(CHIPS):
        out_ref[j] = grads_ref[:, 128 * j : 128 * (j + 1)]
    copies[4].wait()
    y = lax.axis_index("y")
    for i in range(4):
        block = (((y >> 1) ^ i) << 1) | (y & 1)
        rows = pl.ds(pl.multiple_of(block * 16, 16), 16)
        for j in range(CHIPS):
            half_ref[j, 16 * i : 16 * (i + 1), :] = table_ref[rows, 128 * j : 128 * (j + 1)]


def tags(blocks_ref, rows_ref, weights_ref, own_ref, other_ref):
    core = lax.axis_index("core")
    n = 256
    owner = jnp.concatenate([blocks_ref[0:1, :], blocks_ref[1:2, :]], axis=1)
    hot = (owner == iota((64, n), 0)).astype(F32)
    upper = (iota((n, n), 0) < iota((n, n), 1)).astype(BF16)
    before = contract(hot.astype(BF16), upper, 1, 0)
    rank = jnp.sum(before * hot, axis=0, keepdims=True).astype(jnp.int32)
    half = owner & 1
    chip = owner >> 1
    rows = rows_ref[...].astype(F32).astype(BF16)
    rows = jnp.concatenate([rows[:16], rows[16:]], axis=1)
    weights = weights_ref[...].astype(BF16)
    weights = jnp.concatenate([weights[:16], weights[16:]], axis=1)
    entry = iota((CHIPS, n), 1) + 1
    lanes = iota((TAGS, n), 0)
    token_place = (lanes == 2 * CHIPS * CAP + core * CAP + rank).astype(F32).astype(BF16)
    for out, mine in ((own_ref, core), (other_ref, 1 - core)):
        slot = jnp.where(half == mine, core * (CHIPS * CAP) + chip * CAP + rank, -1)
        hits = (lanes == slot).astype(F32).astype(BF16)
        tokens = jnp.where(jnp.where(half == mine, chip, -1) == iota((CHIPS, n), 0), entry, 0)
        tokens = tokens.astype(F32).astype(BF16)
        out_tags = jnp.concatenate([contract(rows, hits, 1, 1), contract(weights, hits, 1, 1)], axis=0)
        out_tags = (out_tags + contract(tokens, token_place, 1, 1)).astype(BF16)
        for i in range(3):
            out[i] = out_tags[:, 128 * i : 128 * (i + 1)]


def first_kernel(own_ref, other_ref, half_ref, out_ref):
    tags = own_ref[...].reshape(96, 128) + other_ref[...].reshape(96, 128)
    for j in range(CHIPS):
        out_ref[j, 0:96, :] = tags
        out_ref[j, 96:160, :] = half_ref[j]


def widen(got_ref, tags_ref, wide_ref):
    for g in range(CHIPS):
        for i in range(3):
            tags_ref[g * 32 : (g + 1) * 32, 128 * i : 128 * (i + 1)] = got_ref[g, 32 * i : 32 * (i + 1), :]
    slot = iota((1, GROUP_SLOTS), 1)
    sender, rank = (slot >> 3) & 1, slot & 7
    used = rank < CAP
    lane = jnp.where(used, sender * (CHIPS * CAP) + (slot >> 4) * CAP + rank, -1)
    spread = (iota((TAGS, GROUP_SLOTS), 0) == lane).astype(F32).astype(BF16)
    lane = jnp.where(used, 2 * CHIPS * CAP - 256 + sender * CAP + rank, -1)
    spread_tokens = (iota((128, GROUP_SLOTS), 0) == lane).astype(F32).astype(BF16)
    for i in range(4):
        rows = slice(256 * i, 256 * (i + 1))
        wide_ref[rows, 0:GROUP_SLOTS] = contract(tags_ref[rows, :], spread, 1, 0)
        wide_ref[rows, GROUP_SLOTS : 2 * GROUP_SLOTS] = contract(
            tags_ref[rows, 256:384], spread_tokens, 1, 0
        )


def token_tags(wide_ref, g, shard_of):
    tokens = wide_ref[pl.ds(pl.multiple_of(g * 32, 32), 32), GROUP_SLOTS : 2 * GROUP_SLOTS]
    tag = jnp.sum(jnp.where(shard_of, tokens, 0.0), axis=0, keepdims=True)
    valid = tag > 0.5
    second_block = (tag > 128.5).astype(F32)
    return valid, tag - 1.0 - 128.0 * second_block, second_block


def slot_rows(wide_ref, g):
    rows = wide_ref[pl.ds(pl.multiple_of(g * 32, 32), 16), 0:GROUP_SLOTS]
    return (rows.astype(jnp.int32) ^ (lax.axis_index("y") * 16)).astype(F32)


def slot_masks():
    core = lax.axis_index("core")
    shard_of = iota((CHIPS, GROUP_SLOTS), 1) // 16 == iota((CHIPS, GROUP_SLOTS), 0)
    second = (iota((1, GROUP_SLOTS), 1) & 8) != 0
    return shard_of, jnp.where(second, 1 - core, core).astype(F32)


def mix_kernel(got_ref, mix_ref, pick_ref, token_ref, tags_ref, wide_ref):
    widen(got_ref, tags_ref, wide_ref)
    shard_of, far = slot_masks()
    position = iota((128, GROUP_SLOTS), 0).astype(F32).astype(BF16)

    def group(g, _):
        valid, token, second_block = token_tags(wide_ref, g, shard_of)
        quarter = (
            (token > 31.5).astype(F32) + (token > 63.5).astype(F32) + (token > 95.5).astype(F32)
        )
        token_ref[g, 0:1, :] = jnp.where(valid, far * 128.0 + token, -1.0)
        token_ref[g, 1:2, :] = jnp.where(valid, far * 32.0 + token - 32.0 * quarter, -1.0)
        part = jnp.where(valid, quarter * 2.0 + second_block, -1.0)
        rows = slot_rows(wide_ref, g)
        picks = jnp.concatenate([jnp.where(part == float(i), rows, -1.0) for i in range(8)], axis=0)
        rows = rows.astype(BF16)
        at = pl.multiple_of(g * 32 + 16, 16)
        weights = wide_ref[pl.ds(at, 16), 0:GROUP_SLOTS].astype(BF16)
        mix = jnp.zeros((128, GROUP_SLOTS), BF16)
        for k in range(16):
            mix = jnp.where(rows[k : k + 1, :] == position, weights[k : k + 1, :], mix)
        here = pl.ds(pl.multiple_of(g * 16, 16), 16)
        mix_ref[:, here, :] = mix.T.reshape(CHIPS, 16, 128)
        pick_ref[:, here, :] = picks.astype(BF16).T.reshape(CHIPS, 16, 128)
        return 0

    lax.fori_loop(0, CHIPS, group, 0, unroll=4)


def table_of(got_ref, table_ref, o):
    pieces = []
    for i in range(4):
        pieces += [got_ref[o, 96 + 16 * i : 112 + 16 * i, :], table_ref[o, 16 * i : 16 * (i + 1), :]]
    return jnp.concatenate(pieces, axis=0)


def add_kernel(near_ref, far_ref, out_ref):
    for j in range(CHIPS):
        out_ref[j] = (near_ref[j].astype(F32) + far_ref[j].astype(F32)).astype(BF16)


def value_kernel(mix_ref, token_ref, got_ref, table_ref, near_ref, far_ref, sums_ref):
    def shard(o, _):
        sums_ref[o] = contract(mix_ref[o], table_of(got_ref, table_ref, o), 1, 0).astype(BF16)
        return 0

    lax.fori_loop(0, CHIPS, shard, 0, unroll=8)
    token_rows = iota((256, GROUP_SLOTS), 0).astype(F32).astype(BF16)

    def group(g, _):
        sums = sums_ref[:, pl.ds(pl.multiple_of(g * 16, 16), 16), :].reshape(GROUP_SLOTS, 128)
        place = token_ref[g, 0:1, :].astype(BF16)
        hits = jnp.where(place == token_rows, jnp.ones((), BF16), jnp.zeros((), BF16))
        out = contract(hits, sums, 1, 0).astype(BF16)
        near_ref[g] = out[:128]
        far_ref[g] = out[128:]
        return 0

    lax.fori_loop(0, CHIPS, group, 0, unroll=8)


def gather_kernel(token_ref, near_ref, far_ref, rows_ref):
    token_rows = iota((256, GROUP_SLOTS), 0).astype(F32).astype(BF16)

    def gather(g, _):
        place = token_ref[g, 0:1, :].astype(BF16)
        hits = jnp.where(place == token_rows, jnp.ones((), BF16), jnp.zeros((), BF16))
        grads = jnp.concatenate([near_ref[g], far_ref[g]], axis=0)
        rows = contract(hits, grads, 0, 0).astype(BF16)
        rows_ref[:, pl.ds(pl.multiple_of(g * 16, 16), 16), :] = rows.reshape(CHIPS, 16, 128)
        return 0

    lax.fori_loop(0, CHIPS, gather, 0, unroll=8)


def table_grad_kernel(mix_ref, rows_ref, keep_ref, send_ref):
    def shard(o, _):
        grad = contract(mix_ref[o], rows_ref[o], 0, 0).astype(BF16)
        for m in range(8):
            (send_ref if m & 1 else keep_ref)[m >> 1, o] = grad[16 * m : 16 * (m + 1)]
        return 0

    lax.fori_loop(0, CHIPS, shard, 0, unroll=8)


def fold_kernel(keep_ref, got_ref, *out_refs):
    for i, out_ref in enumerate(out_refs):
        for j in range(CHIPS):
            out_ref[j] = (keep_ref[i, j].astype(F32) + got_ref[i, j].astype(F32)).astype(BF16)


def weight_grad_kernel(rows_ref, pick_ref, token_ref, got_ref, table_ref, near_ref, far_ref, found_ref):
    def shard(o, _):
        scores = contract(rows_ref[o], table_of(got_ref, table_ref, o), 1, 1)
        picks = pick_ref[o].astype(F32).astype(jnp.int32)
        found = jnp.take_along_axis(scores, jnp.maximum(picks, 0), axis=1, mode="promise_in_bounds")
        found_ref[o] = jnp.where(picks >= 0, found, 0.0).astype(BF16)
        return 0

    lax.fori_loop(0, CHIPS, shard, 0, unroll=8)
    fold_rows = iota((64, GROUP_SLOTS), 0).astype(F32).astype(BF16)

    def group(g, _):
        found = found_ref[:, pl.ds(pl.multiple_of(g * 16, 16), 16), :].reshape(GROUP_SLOTS, 128)
        place = token_ref[g, 1:2, :].astype(BF16)
        hits = jnp.where(place == fold_rows, jnp.ones((), BF16), jnp.zeros((), BF16))
        out = contract(hits, found, 1, 0).astype(BF16)
        near_ref[g] = out[:32]
        far_ref[g] = out[32:]
        return 0

    lax.fori_loop(0, CHIPS, group, 0, unroll=8)


def last_kernel(near_ref, far_ref, *refs):
    out_ref = refs[-1]
    for j in range(CHIPS):
        out_ref[j, 0:32, :] = (near_ref[j].astype(F32) + far_ref[j].astype(F32)).astype(BF16)
        total = refs[0][j].astype(F32)
        for ref in refs[1:-1]:
            total += ref[j].astype(F32)
        out_ref[j, 32:48, :] = total.astype(BF16)


def finish_kernel(got_ref, weight_ref, table_ref):
    def add(j, total):
        return total + got_ref[j, 0:32, :].astype(F32)

    total = lax.fori_loop(0, CHIPS, add, jnp.zeros((32, 128), F32), unroll=8)
    total = jnp.concatenate([total[:, 32 * i : 32 * (i + 1)] for i in range(4)], axis=0)
    weight_ref[...] = total.T.astype(BF16)
    for j in range(CHIPS):
        table_ref[:, 128 * j : 128 * (j + 1)] = got_ref[j, 32:48, :]


def call(kernel, out_shapes, *operands, us=1, scratch=(), limit=16, spaces=()):
    vmem = pl.BlockSpec(memory_space=pltpu.VMEM)
    outs = tuple(s if isinstance(s, jax.ShapeDtypeStruct) else jax.ShapeDtypeStruct(s, BF16) for s in out_shapes)
    return pl.pallas_call(
        kernel,
        out_shape=outs,
        in_specs=[pl.BlockSpec(memory_space=s) for s in spaces] + [vmem] * (len(operands) - len(spaces)),
        out_specs=tuple(vmem for _ in outs),
        scratch_shapes=scratch,
        compiler_params=pltpu.CompilerParams(vmem_limit_bytes=limit * 2**20),
        cost_estimate=pl.CostEstimate(
            flops=0, bytes_accessed=int(us * 3.3e6), transcendentals=0
        ),
    )(*operands)


def swap_cores(v):
    return lax.ppermute(v, "core", [(0, 1), (1, 0)])


def across(v, bits):
    return lax.ppermute(v, "y", [(i, i ^ bits) for i in range(8)])


def exchange(v):
    return lax.all_to_all(v, ("x", "z"), split_axis=0, concat_axis=0, tiled=True)


def after(v, *others):
    return lax.optimization_barrier((v, *others))[0]


def on_device(key_blocks, key_rows, weights, value_table, cotangent):
    own, other, half, grads = call(
        prepare_kernel,
        [(3, 32, 128)] * 2 + [(CHIPS, 64, 128), (CHIPS, 128, 128)],
        key_blocks.T,
        key_rows.T,
        weights.T,
        value_table,
        cotangent,
        us=2,
        scratch=[
            pltpu.VMEM((2, 128), jnp.int32),
            pltpu.VMEM((32, 128), jnp.int32),
            pltpu.VMEM((32, 128), F32),
            pltpu.VMEM((128, 4096), BF16),
            pltpu.VMEM((128, 4096), BF16),
            pltpu.SemaphoreType.DMA((5,)),
        ],
        limit=60,
        spaces=[pl.ANY] * 5,
    )
    other = swap_cores(other)
    (first,) = call(first_kernel, [(CHIPS, 160, 128)], own, other, half, us=0.4)
    got = exchange(first)
    near_grads = exchange(after(grads, got))

    table = across(got[:, 96:, :], 1)
    mix, picks, tokens = call(
        mix_kernel,
        [(CHIPS, GROUP_SLOTS, 128)] * 2 + [jax.ShapeDtypeStruct((CHIPS, 8, GROUP_SLOTS), F32)],
        got,
        us=8.5,
        scratch=[
            pltpu.VMEM((CHIPS * 32, TAGS), BF16),
            pltpu.VMEM((CHIPS * 32, 2 * GROUP_SLOTS), F32),
        ],
    )
    near, far = call(
        value_kernel,
        [(CHIPS, 128, 128)] * 2,
        mix,
        tokens,
        got,
        table,
        us=4.5,
        scratch=[pltpu.VMEM((CHIPS, GROUP_SLOTS, 128), BF16)],
    )
    (out,) = call(add_kernel, [(CHIPS, 128, 128)], near, swap_cores(far), us=0.3)
    got_out = exchange(after(out, near_grads))

    (rows,) = call(
        gather_kernel,
        [(CHIPS, GROUP_SLOTS, 128)],
        tokens,
        near_grads,
        swap_cores(near_grads),
        us=3,
    )
    keep, send = call(table_grad_kernel, [(4, CHIPS, 16, 128)] * 2, mix, rows, us=2.5)
    near, far = call(
        weight_grad_kernel,
        [(CHIPS, 32, 128)] * 2,
        rows,
        picks,
        tokens,
        got,
        table,
        us=8,
        scratch=[pltpu.VMEM((CHIPS, GROUP_SLOTS, 128), BF16)],
    )
    halves = call(fold_kernel, [(CHIPS, 16, 128)] * 4, keep, across(send, 1), us=0.3)
    parts = [halves[0]] + [across(halves[i], 2 * i) for i in (2, 1, 3)]
    (last,) = call(last_kernel, [(CHIPS, 48, 128)], near, swap_cores(far), *parts, us=0.8)
    got_last = exchange(after(last, got_out))
    memory_out = jnp.transpose(got_out, (1, 0, 2)).reshape(128, 4096)
    weight_out, table_out = call(finish_kernel, [(32, 128), (16, 4096)], got_last)
    return memory_out, weight_out.T, table_out


def solution(mesh):
    fine = Mesh(mesh.devices.reshape(4, 8, 2, 8), ("x", "z", "core", "y"))
    tokens = P(("x", "z", "core", "y"), None)
    return jax.shard_map(
        on_device,
        mesh=fine,
        in_specs=(tokens, tokens, tokens, P(("x", "z", "core"), None), tokens),
        out_specs=(tokens, tokens, tokens),
        check_vma=False,
    )
```

```python
import jax
import jax.numpy as jnp
from jax import lax
from jax.experimental import pallas as pl
from jax.experimental.pallas import tpu as pltpu
from jax.sharding import Mesh
from jax.sharding import PartitionSpec as P

CAP = 5
CHIPS = 32
GROUP_SLOTS = 512
TAGS = 384
BF16 = jnp.bfloat16
F32 = jnp.float32


def iota(shape, dim):
    return lax.broadcasted_iota(jnp.int32, shape, dim)


def contract(a, b, da, db):
    return lax.dot_general(a, b, (((da,), (db,)), ((), ())), preferred_element_type=F32)


def prepare_kernel(
    blocks_any,
    rows_any,
    weights_any,
    table_any,
    grads_any,
    own_ref,
    other_ref,
    half_ref,
    out_ref,
    blocks_ref,
    rows_ref,
    weights_ref,
    table_ref,
    grads_ref,
    sems,
):
    anys = (blocks_any, rows_any, weights_any, grads_any, table_any)
    refs = (blocks_ref, rows_ref, weights_ref, grads_ref, table_ref)
    copies = [pltpu.make_async_copy(a, r, sems.at[i]) for i, (a, r) in enumerate(zip(anys, refs))]
    for copy in copies:
        copy.start()
    for copy in copies[:3]:
        copy.wait()
    tags(blocks_ref, rows_ref, weights_ref, own_ref, other_ref)
    copies[3].wait()
    for j in range(CHIPS):
        out_ref[j] = grads_ref[:, 128 * j : 128 * (j + 1)]
    copies[4].wait()
    y = lax.axis_index("y")
    for i in range(4):
        block = (((y >> 1) ^ i) << 1) | (y & 1)
        rows = pl.ds(pl.multiple_of(block * 16, 16), 16)
        for j in range(CHIPS):
            half_ref[j, 16 * i : 16 * (i + 1), :] = table_ref[rows, 128 * j : 128 * (j + 1)]


def tags(blocks_ref, rows_ref, weights_ref, own_ref, other_ref):
    core = lax.axis_index("core")
    n = 256
    owner = jnp.concatenate([blocks_ref[0:1, :], blocks_ref[1:2, :]], axis=1)
    hot = (owner == iota((64, n), 0)).astype(F32)
    upper = (iota((n, n), 0) < iota((n, n), 1)).astype(BF16)
    before = contract(hot.astype(BF16), upper, 1, 0)
    rank = jnp.sum(before * hot, axis=0, keepdims=True).astype(jnp.int32)
    half = owner & 1
    chip = owner >> 1
    rows = rows_ref[...].astype(F32).astype(BF16)
    rows = jnp.concatenate([rows[:16], rows[16:]], axis=1)
    weights = weights_ref[...].astype(BF16)
    weights = jnp.concatenate([weights[:16], weights[16:]], axis=1)
    entry = iota((CHIPS, n), 1) + 1
    lanes = iota((TAGS, n), 0)
    token_place = (lanes == 2 * CHIPS * CAP + core * CAP + rank).astype(F32).astype(BF16)
    for out, mine in ((own_ref, core), (other_ref, 1 - core)):
        slot = jnp.where(half == mine, core * (CHIPS * CAP) + chip * CAP + rank, -1)
        hits = (lanes == slot).astype(F32).astype(BF16)
        tokens = jnp.where(jnp.where(half == mine, chip, -1) == iota((CHIPS, n), 0), entry, 0)
        tokens = tokens.astype(F32).astype(BF16)
        out_tags = jnp.concatenate([contract(rows, hits, 1, 1), contract(weights, hits, 1, 1)], axis=0)
        out_tags = (out_tags + contract(tokens, token_place, 1, 1)).astype(BF16)
        for i in range(3):
            out[i] = out_tags[:, 128 * i : 128 * (i + 1)]


def first_kernel(own_ref, other_ref, half_ref, out_ref):
    tags = own_ref[...].reshape(96, 128) + other_ref[...].reshape(96, 128)
    for j in range(CHIPS):
        out_ref[j, 0:96, :] = tags
        out_ref[j, 96:160, :] = half_ref[j]


def widen(got_ref, tags_ref, wide_ref):
    for g in range(CHIPS):
        for i in range(3):
            tags_ref[g * 32 : (g + 1) * 32, 128 * i : 128 * (i + 1)] = got_ref[g, 32 * i : 32 * (i + 1), :]
    slot = iota((1, GROUP_SLOTS), 1)
    sender, rank = (slot >> 3) & 1, slot & 7
    used = rank < CAP
    lane = jnp.where(used, sender * (CHIPS * CAP) + (slot >> 4) * CAP + rank, -1)
    spread = (iota((TAGS, GROUP_SLOTS), 0) == lane).astype(F32).astype(BF16)
    lane = jnp.where(used, 2 * CHIPS * CAP - 256 + sender * CAP + rank, -1)
    spread_tokens = (iota((128, GROUP_SLOTS), 0) == lane).astype(F32).astype(BF16)
    for i in range(4):
        rows = slice(256 * i, 256 * (i + 1))
        wide_ref[rows, 0:GROUP_SLOTS] = contract(tags_ref[rows, :], spread, 1, 0)
        wide_ref[rows, GROUP_SLOTS : 2 * GROUP_SLOTS] = contract(
            tags_ref[rows, 256:384], spread_tokens, 1, 0
        )


def token_tags(wide_ref, g, shard_of):
    tokens = wide_ref[pl.ds(pl.multiple_of(g * 32, 32), 32), GROUP_SLOTS : 2 * GROUP_SLOTS]
    tag = jnp.sum(jnp.where(shard_of, tokens, 0.0), axis=0, keepdims=True)
    valid = tag > 0.5
    second_block = (tag > 128.5).astype(F32)
    return valid, tag - 1.0 - 128.0 * second_block, second_block


def slot_rows(wide_ref, g):
    rows = wide_ref[pl.ds(pl.multiple_of(g * 32, 32), 16), 0:GROUP_SLOTS]
    return (rows.astype(jnp.int32) ^ (lax.axis_index("y") * 16)).astype(F32)


def slot_masks():
    core = lax.axis_index("core")
    shard_of = iota((CHIPS, GROUP_SLOTS), 1) // 16 == iota((CHIPS, GROUP_SLOTS), 0)
    second = (iota((1, GROUP_SLOTS), 1) & 8) != 0
    return shard_of, jnp.where(second, 1 - core, core).astype(F32)


def mix_kernel(got_ref, mix_ref, pick_ref, token_ref, tags_ref, wide_ref):
    widen(got_ref, tags_ref, wide_ref)
    shard_of, far = slot_masks()
    position = iota((128, GROUP_SLOTS), 0).astype(F32).astype(BF16)

    def group(g, _):
        valid, token, second_block = token_tags(wide_ref, g, shard_of)
        quarter = (
            (token > 31.5).astype(F32) + (token > 63.5).astype(F32) + (token > 95.5).astype(F32)
        )
        token_ref[g, 0:1, :] = jnp.where(valid, far * 128.0 + token, -1.0)
        token_ref[g, 1:2, :] = jnp.where(valid, far * 32.0 + token - 32.0 * quarter, -1.0)
        part = jnp.where(valid, quarter * 2.0 + second_block, -1.0)
        rows = slot_rows(wide_ref, g)
        picks = jnp.concatenate([jnp.where(part == float(i), rows, -1.0) for i in range(8)], axis=0)
        rows = rows.astype(BF16)
        at = pl.multiple_of(g * 32 + 16, 16)
        weights = wide_ref[pl.ds(at, 16), 0:GROUP_SLOTS].astype(BF16)
        mix = jnp.zeros((128, GROUP_SLOTS), BF16)
        for k in range(16):
            mix = jnp.where(rows[k : k + 1, :] == position, weights[k : k + 1, :], mix)
        here = pl.ds(pl.multiple_of(g * 16, 16), 16)
        mix_ref[:, here, :] = mix.T.reshape(CHIPS, 16, 128)
        pick_ref[:, here, :] = picks.astype(BF16).T.reshape(CHIPS, 16, 128)
        return 0

    lax.fori_loop(0, CHIPS, group, 0, unroll=4)


def table_of(got_ref, table_ref, o):
    pieces = []
    for i in range(4):
        pieces += [got_ref[o, 96 + 16 * i : 112 + 16 * i, :], table_ref[o, 16 * i : 16 * (i + 1), :]]
    return jnp.concatenate(pieces, axis=0)


def add_kernel(near_ref, far_ref, out_ref):
    for j in range(CHIPS):
        out_ref[j] = (near_ref[j].astype(F32) + far_ref[j].astype(F32)).astype(BF16)


def value_kernel(mix_ref, token_ref, got_ref, table_ref, near_ref, far_ref, sums_ref):
    def shard(o, _):
        sums_ref[o] = contract(mix_ref[o], table_of(got_ref, table_ref, o), 1, 0).astype(BF16)
        return 0

    lax.fori_loop(0, CHIPS, shard, 0, unroll=8)
    token_rows = iota((256, GROUP_SLOTS), 0).astype(F32).astype(BF16)

    def group(g, _):
        sums = sums_ref[:, pl.ds(pl.multiple_of(g * 16, 16), 16), :].reshape(GROUP_SLOTS, 128)
        place = token_ref[g, 0:1, :].astype(BF16)
        hits = jnp.where(place == token_rows, jnp.ones((), BF16), jnp.zeros((), BF16))
        out = contract(hits, sums, 1, 0).astype(BF16)
        near_ref[g] = out[:128]
        far_ref[g] = out[128:]
        return 0

    lax.fori_loop(0, CHIPS, group, 0, unroll=8)


def gather_kernel(token_ref, near_ref, far_ref, rows_ref):
    token_rows = iota((256, GROUP_SLOTS), 0).astype(F32).astype(BF16)

    def gather(g, _):
        place = token_ref[g, 0:1, :].astype(BF16)
        hits = jnp.where(place == token_rows, jnp.ones((), BF16), jnp.zeros((), BF16))
        grads = jnp.concatenate([near_ref[g], far_ref[g]], axis=0)
        rows = contract(hits, grads, 0, 0).astype(BF16)
        rows_ref[:, pl.ds(pl.multiple_of(g * 16, 16), 16), :] = rows.reshape(CHIPS, 16, 128)
        return 0

    lax.fori_loop(0, CHIPS, gather, 0, unroll=8)


def table_grad_kernel(mix_ref, rows_ref, keep_ref, send_ref):
    def shard(o, _):
        grad = contract(mix_ref[o], rows_ref[o], 0, 0).astype(BF16)
        for m in range(8):
            (send_ref if m & 1 else keep_ref)[m >> 1, o] = grad[16 * m : 16 * (m + 1)]
        return 0

    lax.fori_loop(0, CHIPS, shard, 0, unroll=8)


def fold_kernel(keep_ref, got_ref, *out_refs):
    for i, out_ref in enumerate(out_refs):
        for j in range(CHIPS):
            out_ref[j] = (keep_ref[i, j].astype(F32) + got_ref[i, j].astype(F32)).astype(BF16)


def weight_grad_kernel(rows_ref, pick_ref, token_ref, got_ref, table_ref, near_ref, far_ref, found_ref):
    def shard(o, _):
        scores = contract(rows_ref[o], table_of(got_ref, table_ref, o), 1, 1)
        picks = pick_ref[o].astype(F32).astype(jnp.int32)
        found = jnp.take_along_axis(scores, jnp.maximum(picks, 0), axis=1, mode="promise_in_bounds")
        found_ref[o] = jnp.where(picks >= 0, found, 0.0).astype(BF16)
        return 0

    lax.fori_loop(0, CHIPS, shard, 0, unroll=8)
    fold_rows = iota((64, GROUP_SLOTS), 0).astype(F32).astype(BF16)

    def group(g, _):
        found = found_ref[:, pl.ds(pl.multiple_of(g * 16, 16), 16), :].reshape(GROUP_SLOTS, 128)
        place = token_ref[g, 1:2, :].astype(BF16)
        hits = jnp.where(place == fold_rows, jnp.ones((), BF16), jnp.zeros((), BF16))
        out = contract(hits, found, 1, 0).astype(BF16)
        near_ref[g] = out[:32]
        far_ref[g] = out[32:]
        return 0

    lax.fori_loop(0, CHIPS, group, 0, unroll=8)


def last_kernel(near_ref, far_ref, *refs):
    out_ref = refs[-1]
    for j in range(CHIPS):
        out_ref[j, 0:32, :] = (near_ref[j].astype(F32) + far_ref[j].astype(F32)).astype(BF16)
        total = refs[0][j].astype(F32)
        for ref in refs[1:-1]:
            total += ref[j].astype(F32)
        out_ref[j, 32:48, :] = total.astype(BF16)


def finish_kernel(got_ref, weight_ref, table_ref):
    def add(j, total):
        return total + got_ref[j, 0:32, :].astype(F32)

    total = lax.fori_loop(0, CHIPS, add, jnp.zeros((32, 128), F32), unroll=8)
    total = jnp.concatenate([total[:, 32 * i : 32 * (i + 1)] for i in range(4)], axis=0)
    weight_ref[...] = total.T.astype(BF16)
    for j in range(CHIPS):
        table_ref[:, 128 * j : 128 * (j + 1)] = got_ref[j, 32:48, :]


def call(kernel, out_shapes, *operands, us=1, scratch=(), limit=16, spaces=()):
    vmem = pl.BlockSpec(memory_space=pltpu.VMEM)
    outs = tuple(s if isinstance(s, jax.ShapeDtypeStruct) else jax.ShapeDtypeStruct(s, BF16) for s in out_shapes)
    return pl.pallas_call(
        kernel,
        out_shape=outs,
        in_specs=[pl.BlockSpec(memory_space=s) for s in spaces] + [vmem] * (len(operands) - len(spaces)),
        out_specs=tuple(vmem for _ in outs),
        scratch_shapes=scratch,
        compiler_params=pltpu.CompilerParams(vmem_limit_bytes=limit * 2**20),
        cost_estimate=pl.CostEstimate(
            flops=int(us * 1e9), bytes_accessed=int(us * 3.3e6), transcendentals=0
        ),
    )(*operands)


def swap_cores(v):
    return lax.ppermute(v, "core", [(0, 1), (1, 0)])


def across(v, bits):
    return lax.ppermute(v, "y", [(i, i ^ bits) for i in range(8)])


def exchange(v):
    return lax.all_to_all(v, ("x", "z"), split_axis=0, concat_axis=0, tiled=True)


def after(v, *others):
    return lax.optimization_barrier((v, *others))[0]


def on_device(key_blocks, key_rows, weights, value_table, cotangent):
    own, other, half, grads = call(
        prepare_kernel,
        [(3, 32, 128)] * 2 + [(CHIPS, 64, 128), (CHIPS, 128, 128)],
        key_blocks.T,
        key_rows.T,
        weights.T,
        value_table,
        cotangent,
        us=2,
        scratch=[
            pltpu.VMEM((2, 128), jnp.int32),
            pltpu.VMEM((32, 128), jnp.int32),
            pltpu.VMEM((32, 128), F32),
            pltpu.VMEM((128, 4096), BF16),
            pltpu.VMEM((128, 4096), BF16),
            pltpu.SemaphoreType.DMA((5,)),
        ],
        limit=60,
        spaces=[pl.ANY] * 5,
    )
    other = swap_cores(other)
    (first,) = call(first_kernel, [(CHIPS, 160, 128)], own, other, half, us=0.4)
    got = exchange(first)
    near_grads = exchange(after(grads, got))

    table = across(got[:, 96:, :], 1)
    mix, picks, tokens = call(
        mix_kernel,
        [(CHIPS, GROUP_SLOTS, 128)] * 2 + [jax.ShapeDtypeStruct((CHIPS, 8, GROUP_SLOTS), F32)],
        got,
        us=8.5,
        scratch=[
            pltpu.VMEM((CHIPS * 32, TAGS), BF16),
            pltpu.VMEM((CHIPS * 32, 2 * GROUP_SLOTS), F32),
        ],
    )
    near, far = call(
        value_kernel,
        [(CHIPS, 128, 128)] * 2,
        mix,
        tokens,
        got,
        table,
        us=4.5,
        scratch=[pltpu.VMEM((CHIPS, GROUP_SLOTS, 128), BF16)],
    )
    (out,) = call(add_kernel, [(CHIPS, 128, 128)], near, swap_cores(far), us=0.3)
    got_out = exchange(after(out, near_grads))

    (rows,) = call(
        gather_kernel,
        [(CHIPS, GROUP_SLOTS, 128)],
        tokens,
        near_grads,
        swap_cores(near_grads),
        us=3,
    )
    keep, send = call(table_grad_kernel, [(4, CHIPS, 16, 128)] * 2, mix, rows, us=2.5)
    near, far = call(
        weight_grad_kernel,
        [(CHIPS, 32, 128)] * 2,
        rows,
        picks,
        tokens,
        got,
        table,
        us=8,
        scratch=[pltpu.VMEM((CHIPS, GROUP_SLOTS, 128), BF16)],
    )
    halves = call(fold_kernel, [(CHIPS, 16, 128)] * 4, keep, across(send, 1), us=0.3)
    parts = [halves[0]] + [across(halves[i], 2 * i) for i in (2, 1, 3)]
    (last,) = call(last_kernel, [(CHIPS, 48, 128)], near, swap_cores(far), *parts, us=0.8)
    got_last = exchange(after(last, got_out))
    memory_out = jnp.transpose(got_out, (1, 0, 2)).reshape(128, 4096)
    weight_out, table_out = call(finish_kernel, [(32, 128), (16, 4096)], got_last)
    return memory_out, weight_out.T, table_out


def solution(mesh):
    fine = Mesh(mesh.devices.reshape(4, 8, 2, 8), ("x", "z", "core", "y"))
    tokens = P(("x", "z", "core", "y"), None)
    return jax.shard_map(
        on_device,
        mesh=fine,
        in_specs=(tokens, tokens, tokens, P(("x", "z", "core"), None), tokens),
        out_specs=(tokens, tokens, tokens),
        check_vma=False,
    )
```

```python
import jax
import jax.numpy as jnp
from jax import lax
from jax.experimental import pallas as pl
from jax.experimental.pallas import tpu as pltpu
from jax.sharding import Mesh
from jax.sharding import PartitionSpec as P

CAP = 5
CHIPS = 32
GROUP_SLOTS = 512
TAGS = 384
BF16 = jnp.bfloat16
F32 = jnp.float32


def iota(shape, dim):
    return lax.broadcasted_iota(jnp.int32, shape, dim)


def contract(a, b, da, db):
    return lax.dot_general(a, b, (((da,), (db,)), ((), ())), preferred_element_type=F32)


def prepare_kernel(
    blocks_any,
    rows_any,
    weights_any,
    table_any,
    grads_any,
    own_ref,
    other_ref,
    half_ref,
    out_ref,
    blocks_ref,
    rows_ref,
    weights_ref,
    table_ref,
    grads_ref,
    sems,
):
    anys = (blocks_any, rows_any, weights_any, grads_any, table_any)
    refs = (blocks_ref, rows_ref, weights_ref, grads_ref, table_ref)
    copies = [pltpu.make_async_copy(a, r, sems.at[i]) for i, (a, r) in enumerate(zip(anys, refs))]
    for copy in copies:
        copy.start()
    for copy in copies[:3]:
        copy.wait()
    tags(blocks_ref, rows_ref, weights_ref, own_ref, other_ref)
    copies[3].wait()
    for j in range(CHIPS):
        out_ref[j] = grads_ref[:, 128 * j : 128 * (j + 1)]
    copies[4].wait()
    y = lax.axis_index("y")
    for i in range(4):
        block = (((y >> 1) ^ i) << 1) | (y & 1)
        rows = pl.ds(pl.multiple_of(block * 16, 16), 16)
        for j in range(CHIPS):
            half_ref[j, 16 * i : 16 * (i + 1), :] = table_ref[rows, 128 * j : 128 * (j + 1)]


def tags(blocks_ref, rows_ref, weights_ref, own_ref, other_ref):
    core = lax.axis_index("core")
    n = 256
    owner = jnp.concatenate([blocks_ref[0:1, :], blocks_ref[1:2, :]], axis=1)
    hot = (owner == iota((64, n), 0)).astype(F32)
    upper = (iota((n, n), 0) < iota((n, n), 1)).astype(BF16)
    before = contract(hot.astype(BF16), upper, 1, 0)
    rank = jnp.sum(before * hot, axis=0, keepdims=True).astype(jnp.int32)
    half = owner & 1
    chip = owner >> 1
    rows = rows_ref[...].astype(F32).astype(BF16)
    rows = jnp.concatenate([rows[:16], rows[16:]], axis=1)
    weights = weights_ref[...].astype(BF16)
    weights = jnp.concatenate([weights[:16], weights[16:]], axis=1)
    entry = iota((CHIPS, n), 1) + 1
    lanes = iota((TAGS, n), 0)
    token_place = (lanes == 2 * CHIPS * CAP + core * CAP + rank).astype(F32).astype(BF16)
    for out, mine in ((own_ref, core), (other_ref, 1 - core)):
        slot = jnp.where(half == mine, core * (CHIPS * CAP) + chip * CAP + rank, -1)
        hits = (lanes == slot).astype(F32).astype(BF16)
        tokens = jnp.where(jnp.where(half == mine, chip, -1) == iota((CHIPS, n), 0), entry, 0)
        tokens = tokens.astype(F32).astype(BF16)
        out_tags = jnp.concatenate([contract(rows, hits, 1, 1), contract(weights, hits, 1, 1)], axis=0)
        out_tags = (out_tags + contract(tokens, token_place, 1, 1)).astype(BF16)
        for i in range(3):
            out[i] = out_tags[:, 128 * i : 128 * (i + 1)]


def first_kernel(own_ref, other_ref, half_ref, out_ref):
    tags = own_ref[...].reshape(96, 128) + other_ref[...].reshape(96, 128)
    for j in range(CHIPS):
        out_ref[j, 0:96, :] = tags
        out_ref[j, 96:160, :] = half_ref[j]


def widen(got_ref, tags_ref, wide_ref):
    for g in range(CHIPS):
        for i in range(3):
            tags_ref[g * 32 : (g + 1) * 32, 128 * i : 128 * (i + 1)] = got_ref[g, 32 * i : 32 * (i + 1), :]
    slot = iota((1, GROUP_SLOTS), 1)
    sender, rank = (slot >> 3) & 1, slot & 7
    used = rank < CAP
    lane = jnp.where(used, sender * (CHIPS * CAP) + (slot >> 4) * CAP + rank, -1)
    spread = (iota((TAGS, GROUP_SLOTS), 0) == lane).astype(F32).astype(BF16)
    lane = jnp.where(used, 2 * CHIPS * CAP - 256 + sender * CAP + rank, -1)
    spread_tokens = (iota((128, GROUP_SLOTS), 0) == lane).astype(F32).astype(BF16)
    for i in range(4):
        rows = slice(256 * i, 256 * (i + 1))
        wide_ref[rows, 0:GROUP_SLOTS] = contract(tags_ref[rows, :], spread, 1, 0)
        wide_ref[rows, GROUP_SLOTS : 2 * GROUP_SLOTS] = contract(
            tags_ref[rows, 256:384], spread_tokens, 1, 0
        )


def token_tags(wide_ref, g, shard_of):
    tokens = wide_ref[pl.ds(pl.multiple_of(g * 32, 32), 32), GROUP_SLOTS : 2 * GROUP_SLOTS]
    tag = jnp.sum(jnp.where(shard_of, tokens, 0.0), axis=0, keepdims=True)
    valid = tag > 0.5
    second_block = (tag > 128.5).astype(F32)
    return valid, tag - 1.0 - 128.0 * second_block, second_block


def slot_rows(wide_ref, g):
    rows = wide_ref[pl.ds(pl.multiple_of(g * 32, 32), 16), 0:GROUP_SLOTS]
    return (rows.astype(jnp.int32) ^ (lax.axis_index("y") * 16)).astype(F32)


def slot_masks():
    core = lax.axis_index("core")
    shard_of = iota((CHIPS, GROUP_SLOTS), 1) // 16 == iota((CHIPS, GROUP_SLOTS), 0)
    second = (iota((1, GROUP_SLOTS), 1) & 8) != 0
    return shard_of, jnp.where(second, 1 - core, core).astype(F32)


def mix_kernel(got_ref, mix_ref, pick_ref, token_ref, tags_ref, wide_ref):
    widen(got_ref, tags_ref, wide_ref)
    shard_of, far = slot_masks()
    position = iota((128, GROUP_SLOTS), 0).astype(F32).astype(BF16)

    def group(g, _):
        valid, token, second_block = token_tags(wide_ref, g, shard_of)
        quarter = (
            (token > 31.5).astype(F32) + (token > 63.5).astype(F32) + (token > 95.5).astype(F32)
        )
        token_ref[g, 0:1, :] = jnp.where(valid, far * 128.0 + token, -1.0)
        token_ref[g, 1:2, :] = jnp.where(valid, far * 32.0 + token - 32.0 * quarter, -1.0)
        part = jnp.where(valid, quarter * 2.0 + second_block, -1.0)
        rows = slot_rows(wide_ref, g)
        picks = jnp.concatenate([jnp.where(part == float(i), rows, -1.0) for i in range(8)], axis=0)
        rows = rows.astype(BF16)
        at = pl.multiple_of(g * 32 + 16, 16)
        weights = wide_ref[pl.ds(at, 16), 0:GROUP_SLOTS].astype(BF16)
        mix = jnp.zeros((128, GROUP_SLOTS), BF16)
        for k in range(16):
            mix = jnp.where(rows[k : k + 1, :] == position, weights[k : k + 1, :], mix)
        here = pl.ds(pl.multiple_of(g * 16, 16), 16)
        mix_ref[:, here, :] = mix.T.reshape(CHIPS, 16, 128)
        pick_ref[:, here, :] = picks.astype(BF16).T.reshape(CHIPS, 16, 128)
        return 0

    lax.fori_loop(0, CHIPS, group, 0, unroll=4)


def table_of(got_ref, table_ref, o):
    pieces = []
    for i in range(4):
        pieces += [got_ref[o, 96 + 16 * i : 112 + 16 * i, :], table_ref[o, 16 * i : 16 * (i + 1), :]]
    return jnp.concatenate(pieces, axis=0)


def add_kernel(near_ref, far_ref, out_ref):
    for j in range(CHIPS):
        out_ref[j] = (near_ref[j].astype(F32) + far_ref[j].astype(F32)).astype(BF16)


def value_kernel(mix_ref, token_ref, got_ref, table_ref, near_ref, far_ref, sums_ref):
    def shard(o, _):
        sums_ref[o] = contract(mix_ref[o], table_of(got_ref, table_ref, o), 1, 0).astype(BF16)
        return 0

    lax.fori_loop(0, CHIPS, shard, 0, unroll=8)
    token_rows = iota((256, GROUP_SLOTS), 0).astype(F32).astype(BF16)

    def group(g, _):
        sums = sums_ref[:, pl.ds(pl.multiple_of(g * 16, 16), 16), :].reshape(GROUP_SLOTS, 128)
        place = token_ref[g, 0:1, :].astype(BF16)
        hits = jnp.where(place == token_rows, jnp.ones((), BF16), jnp.zeros((), BF16))
        out = contract(hits, sums, 1, 0).astype(BF16)
        near_ref[g] = out[:128]
        far_ref[g] = out[128:]
        return 0

    lax.fori_loop(0, CHIPS, group, 0, unroll=8)


def gather_kernel(near_any, far_any, token_ref, rows_ref, near_ref, far_ref, sems):
    chunk = CHIPS // 4
    copies = []
    for i in range(4):
        part = pl.ds(i * chunk, chunk)
        for j, (source, ref) in enumerate(((near_any, near_ref), (far_any, far_ref))):
            copies.append(pltpu.make_async_copy(source.at[part], ref.at[part], sems.at[2 * i + j]))
    for copy in copies:
        copy.start()
    token_rows = iota((256, GROUP_SLOTS), 0).astype(F32).astype(BF16)

    def gather(g, _):
        place = token_ref[g, 0:1, :].astype(BF16)
        hits = jnp.where(place == token_rows, jnp.ones((), BF16), jnp.zeros((), BF16))
        grads = jnp.concatenate([near_ref[g], far_ref[g]], axis=0)
        rows = contract(hits, grads, 0, 0).astype(BF16)
        rows_ref[:, pl.ds(pl.multiple_of(g * 16, 16), 16), :] = rows.reshape(CHIPS, 16, 128)
        return 0

    for i in range(4):
        copies[2 * i].wait()
        copies[2 * i + 1].wait()
        lax.fori_loop(i * chunk, (i + 1) * chunk, gather, 0, unroll=8)


def table_grad_kernel(mix_ref, rows_ref, keep_ref, send_ref):
    def shard(o, _):
        grad = contract(mix_ref[o], rows_ref[o], 0, 0).astype(BF16)
        for m in range(8):
            (send_ref if m & 1 else keep_ref)[m >> 1, o] = grad[16 * m : 16 * (m + 1)]
        return 0

    lax.fori_loop(0, CHIPS, shard, 0, unroll=8)


def fold_kernel(keep_ref, got_ref, *out_refs):
    for i, out_ref in enumerate(out_refs):
        for j in range(CHIPS):
            out_ref[j] = (keep_ref[i, j].astype(F32) + got_ref[i, j].astype(F32)).astype(BF16)


def weight_grad_kernel(rows_ref, pick_ref, token_ref, got_ref, table_ref, near_ref, far_ref, found_ref):
    def shard(o, _):
        scores = contract(rows_ref[o], table_of(got_ref, table_ref, o), 1, 1)
        picks = pick_ref[o].astype(F32).astype(jnp.int32)
        found = jnp.take_along_axis(scores, jnp.maximum(picks, 0), axis=1, mode="promise_in_bounds")
        found_ref[o] = jnp.where(picks >= 0, found, 0.0).astype(BF16)
        return 0

    lax.fori_loop(0, CHIPS, shard, 0, unroll=8)
    fold_rows = iota((64, GROUP_SLOTS), 0).astype(F32).astype(BF16)

    def group(g, _):
        found = found_ref[:, pl.ds(pl.multiple_of(g * 16, 16), 16), :].reshape(GROUP_SLOTS, 128)
        place = token_ref[g, 1:2, :].astype(BF16)
        hits = jnp.where(place == fold_rows, jnp.ones((), BF16), jnp.zeros((), BF16))
        out = contract(hits, found, 1, 0).astype(BF16)
        near_ref[g] = out[:32]
        far_ref[g] = out[32:]
        return 0

    lax.fori_loop(0, CHIPS, group, 0, unroll=8)


def last_kernel(near_ref, far_ref, *refs):
    out_ref = refs[-1]
    for j in range(CHIPS):
        out_ref[j, 0:32, :] = (near_ref[j].astype(F32) + far_ref[j].astype(F32)).astype(BF16)
        total = refs[0][j].astype(F32)
        for ref in refs[1:-1]:
            total += ref[j].astype(F32)
        out_ref[j, 32:48, :] = total.astype(BF16)


def finish_kernel(got_ref, weight_ref, table_ref):
    def add(j, total):
        return total + got_ref[j, 0:32, :].astype(F32)

    total = lax.fori_loop(0, CHIPS, add, jnp.zeros((32, 128), F32), unroll=8)
    total = jnp.concatenate([total[:, 32 * i : 32 * (i + 1)] for i in range(4)], axis=0)
    weight_ref[...] = total.T.astype(BF16)
    for j in range(CHIPS):
        table_ref[:, 128 * j : 128 * (j + 1)] = got_ref[j, 32:48, :]


def call(kernel, out_shapes, *operands, us=1, scratch=(), limit=16, spaces=()):
    vmem = pl.BlockSpec(memory_space=pltpu.VMEM)
    outs = tuple(s if isinstance(s, jax.ShapeDtypeStruct) else jax.ShapeDtypeStruct(s, BF16) for s in out_shapes)
    return pl.pallas_call(
        kernel,
        out_shape=outs,
        in_specs=[pl.BlockSpec(memory_space=s) for s in spaces] + [vmem] * (len(operands) - len(spaces)),
        out_specs=tuple(vmem for _ in outs),
        scratch_shapes=scratch,
        compiler_params=pltpu.CompilerParams(vmem_limit_bytes=limit * 2**20),
        cost_estimate=pl.CostEstimate(
            flops=int(us * 1e9), bytes_accessed=int(us * 3.3e6), transcendentals=0
        ),
    )(*operands)


def swap_cores(v):
    return lax.ppermute(v, "core", [(0, 1), (1, 0)])


def across(v, bits):
    return lax.ppermute(v, "y", [(i, i ^ bits) for i in range(8)])


def exchange(v):
    return lax.all_to_all(v, ("x", "z"), split_axis=0, concat_axis=0, tiled=True)


def after(v, *others):
    return lax.optimization_barrier((v, *others))[0]


def on_device(key_blocks, key_rows, weights, value_table, cotangent):
    own, other, half, grads = call(
        prepare_kernel,
        [(3, 32, 128)] * 2 + [(CHIPS, 64, 128), (CHIPS, 128, 128)],
        key_blocks.T,
        key_rows.T,
        weights.T,
        value_table,
        cotangent,
        us=2,
        scratch=[
            pltpu.VMEM((2, 128), jnp.int32),
            pltpu.VMEM((32, 128), jnp.int32),
            pltpu.VMEM((32, 128), F32),
            pltpu.VMEM((128, 4096), BF16),
            pltpu.VMEM((128, 4096), BF16),
            pltpu.SemaphoreType.DMA((5,)),
        ],
        limit=60,
        spaces=[pl.ANY] * 5,
    )
    other = swap_cores(other)
    (first,) = call(first_kernel, [(CHIPS, 160, 128)], own, other, half, us=0.4)
    got = exchange(first)
    near_grads = exchange(after(grads, got))

    table = across(got[:, 96:, :], 1)
    mix, picks, tokens = call(
        mix_kernel,
        [(CHIPS, GROUP_SLOTS, 128)] * 2 + [jax.ShapeDtypeStruct((CHIPS, 8, GROUP_SLOTS), F32)],
        got,
        us=8.5,
        scratch=[
            pltpu.VMEM((CHIPS * 32, TAGS), BF16),
            pltpu.VMEM((CHIPS * 32, 2 * GROUP_SLOTS), F32),
        ],
    )
    near, far = call(
        value_kernel,
        [(CHIPS, 128, 128)] * 2,
        mix,
        tokens,
        got,
        table,
        us=4.5,
        scratch=[pltpu.VMEM((CHIPS, GROUP_SLOTS, 128), BF16)],
    )
    (out,) = call(add_kernel, [(CHIPS, 128, 128)], near, swap_cores(far), us=0.3)
    got_out = exchange(after(out, near_grads))

    (rows,) = call(
        gather_kernel,
        [(CHIPS, GROUP_SLOTS, 128)],
        near_grads,
        swap_cores(near_grads),
        tokens,
        us=3,
        scratch=[
            pltpu.VMEM((CHIPS, 128, 128), BF16),
            pltpu.VMEM((CHIPS, 128, 128), BF16),
            pltpu.SemaphoreType.DMA((8,)),
        ],
        spaces=[pl.ANY] * 2,
    )
    keep, send = call(table_grad_kernel, [(4, CHIPS, 16, 128)] * 2, mix, rows, us=2.5)
    near, far = call(
        weight_grad_kernel,
        [(CHIPS, 32, 128)] * 2,
        rows,
        picks,
        tokens,
        got,
        table,
        us=8,
        scratch=[pltpu.VMEM((CHIPS, GROUP_SLOTS, 128), BF16)],
    )
    halves = call(fold_kernel, [(CHIPS, 16, 128)] * 4, keep, across(send, 1), us=0.3)
    parts = [halves[0]] + [across(halves[i], 2 * i) for i in (2, 1, 3)]
    (last,) = call(last_kernel, [(CHIPS, 48, 128)], near, swap_cores(far), *parts, us=0.8)
    got_last = exchange(after(last, got_out))
    memory_out = jnp.transpose(got_out, (1, 0, 2)).reshape(128, 4096)
    weight_out, table_out = call(finish_kernel, [(32, 128), (16, 4096)], got_last)
    return memory_out, weight_out.T, table_out


def solution(mesh):
    fine = Mesh(mesh.devices.reshape(4, 8, 2, 8), ("x", "z", "core", "y"))
    tokens = P(("x", "z", "core", "y"), None)
    return jax.shard_map(
        on_device,
        mesh=fine,
        in_specs=(tokens, tokens, tokens, P(("x", "z", "core"), None), tokens),
        out_specs=(tokens, tokens, tokens),
        check_vma=False,
    )
```

```python
import jax
import jax.numpy as jnp
from jax import lax
from jax.experimental import pallas as pl
from jax.experimental.pallas import tpu as pltpu
from jax.sharding import Mesh
from jax.sharding import PartitionSpec as P

CAP = 5
CHIPS = 32
GROUP_SLOTS = 512
TAGS = 384
BF16 = jnp.bfloat16
F32 = jnp.float32


def iota(shape, dim):
    return lax.broadcasted_iota(jnp.int32, shape, dim)


def contract(a, b, da, db):
    return lax.dot_general(a, b, (((da,), (db,)), ((), ())), preferred_element_type=F32)


def fetch(sources, refs, sems):
    copies = [pltpu.make_async_copy(a, r, sems.at[i]) for i, (a, r) in enumerate(zip(sources, refs))]
    for copy in copies:
        copy.start()
    return copies


def tag_kernel(blocks_any, rows_any, weights_any, own_ref, other_ref, blocks_ref, rows_ref, weights_ref, sems):
    copies = fetch(
        (blocks_any, rows_any, weights_any), (blocks_ref, rows_ref, weights_ref), sems
    )
    for copy in copies:
        copy.wait()
    tags(blocks_ref, rows_ref, weights_ref, own_ref, other_ref)


def body_kernel(grads_any, table_any, half_ref, out_ref, grads_ref, table_ref, sems):
    copies = fetch((table_any, grads_any), (table_ref, grads_ref), sems)
    y = lax.axis_index("y")
    copies[0].wait()
    for i in range(4):
        block = (((y >> 1) ^ i) << 1) | (y & 1)
        rows = pl.ds(pl.multiple_of(block * 16, 16), 16)
        for j in range(CHIPS):
            half_ref[j, 16 * i : 16 * (i + 1), :] = table_ref[rows, 128 * j : 128 * (j + 1)]
    copies[1].wait()
    for j in range(CHIPS):
        out_ref[j] = grads_ref[:, 128 * j : 128 * (j + 1)]


def tags(blocks_ref, rows_ref, weights_ref, own_ref, other_ref):
    core = lax.axis_index("core")
    n = 256
    owner = jnp.concatenate([blocks_ref[0:1, :], blocks_ref[1:2, :]], axis=1)
    hot = (owner == iota((64, n), 0)).astype(F32)
    upper = (iota((n, n), 0) < iota((n, n), 1)).astype(BF16)
    before = contract(hot.astype(BF16), upper, 1, 0)
    rank = jnp.sum(before * hot, axis=0, keepdims=True).astype(jnp.int32)
    half = owner & 1
    chip = owner >> 1
    rows = rows_ref[...].astype(F32).astype(BF16)
    rows = jnp.concatenate([rows[:16], rows[16:]], axis=1)
    weights = weights_ref[...].astype(BF16)
    weights = jnp.concatenate([weights[:16], weights[16:]], axis=1)
    entry = iota((CHIPS, n), 1) + 1
    lanes = iota((TAGS, n), 0)
    token_place = (lanes == 2 * CHIPS * CAP + core * CAP + rank).astype(F32).astype(BF16)
    for out, mine in ((own_ref, core), (other_ref, 1 - core)):
        slot = jnp.where(half == mine, core * (CHIPS * CAP) + chip * CAP + rank, -1)
        hits = (lanes == slot).astype(F32).astype(BF16)
        tokens = jnp.where(jnp.where(half == mine, chip, -1) == iota((CHIPS, n), 0), entry, 0)
        tokens = tokens.astype(F32).astype(BF16)
        out_tags = jnp.concatenate([contract(rows, hits, 1, 1), contract(weights, hits, 1, 1)], axis=0)
        out_tags = (out_tags + contract(tokens, token_place, 1, 1)).astype(BF16)
        for i in range(3):
            out[i] = out_tags[:, 128 * i : 128 * (i + 1)]


def first_kernel(own_ref, other_ref, half_ref, out_ref):
    both = own_ref[...].reshape(96, 128) + other_ref[...].reshape(96, 128)
    for j in range(CHIPS):
        out_ref[j, 0:96, :] = both
        out_ref[j, 96:160, :] = half_ref[j]


def widen(got_ref, tags_ref, wide_ref):
    for g in range(CHIPS):
        for i in range(3):
            tags_ref[g * 32 : (g + 1) * 32, 128 * i : 128 * (i + 1)] = got_ref[g, 32 * i : 32 * (i + 1), :]
    slot = iota((1, GROUP_SLOTS), 1)
    sender, rank = (slot >> 3) & 1, slot & 7
    used = rank < CAP
    lane = jnp.where(used, sender * (CHIPS * CAP) + (slot >> 4) * CAP + rank, -1)
    spread = (iota((TAGS, GROUP_SLOTS), 0) == lane).astype(F32).astype(BF16)
    lane = jnp.where(used, 2 * CHIPS * CAP - 256 + sender * CAP + rank, -1)
    spread_tokens = (iota((128, GROUP_SLOTS), 0) == lane).astype(F32).astype(BF16)
    for i in range(4):
        rows = slice(256 * i, 256 * (i + 1))
        wide_ref[rows, 0:GROUP_SLOTS] = contract(tags_ref[rows, :], spread, 1, 0)
        wide_ref[rows, GROUP_SLOTS : 2 * GROUP_SLOTS] = contract(
            tags_ref[rows, 256:384], spread_tokens, 1, 0
        )


def token_tags(wide_ref, g, shard_of):
    tokens = wide_ref[pl.ds(pl.multiple_of(g * 32, 32), 32), GROUP_SLOTS : 2 * GROUP_SLOTS]
    tag = jnp.sum(jnp.where(shard_of, tokens, 0.0), axis=0, keepdims=True)
    valid = tag > 0.5
    second_block = (tag > 128.5).astype(F32)
    return valid, tag - 1.0 - 128.0 * second_block, second_block


def slot_rows(wide_ref, g):
    rows = wide_ref[pl.ds(pl.multiple_of(g * 32, 32), 16), 0:GROUP_SLOTS]
    return (rows.astype(jnp.int32) ^ (lax.axis_index("y") * 16)).astype(F32)


def slot_masks():
    core = lax.axis_index("core")
    shard_of = iota((CHIPS, GROUP_SLOTS), 1) // 16 == iota((CHIPS, GROUP_SLOTS), 0)
    second = (iota((1, GROUP_SLOTS), 1) & 8) != 0
    return shard_of, jnp.where(second, 1 - core, core).astype(F32)


def mix_kernel(got_ref, mix_ref, pick_ref, token_ref, tags_ref, wide_ref):
    widen(got_ref, tags_ref, wide_ref)
    shard_of, far = slot_masks()
    position = iota((128, GROUP_SLOTS), 0).astype(F32).astype(BF16)

    def group(g, _):
        valid, token, second_block = token_tags(wide_ref, g, shard_of)
        quarter = (
            (token > 31.5).astype(F32) + (token > 63.5).astype(F32) + (token > 95.5).astype(F32)
        )
        token_ref[g, 0:1, :] = jnp.where(valid, far * 128.0 + token, -1.0)
        token_ref[g, 1:2, :] = jnp.where(valid, far * 32.0 + token - 32.0 * quarter, -1.0)
        part = jnp.where(valid, quarter * 2.0 + second_block, -1.0)
        rows = slot_rows(wide_ref, g)
        picks = jnp.concatenate([jnp.where(part == float(i), rows, -1.0) for i in range(8)], axis=0)
        rows = rows.astype(BF16)
        at = pl.multiple_of(g * 32 + 16, 16)
        weights = wide_ref[pl.ds(at, 16), 0:GROUP_SLOTS].astype(BF16)
        mix = jnp.zeros((128, GROUP_SLOTS), BF16)
        for k in range(16):
            mix = jnp.where(rows[k : k + 1, :] == position, weights[k : k + 1, :], mix)
        here = pl.ds(pl.multiple_of(g * 16, 16), 16)
        mix_ref[:, here, :] = mix.T.reshape(CHIPS, 16, 128)
        pick_ref[:, here, :] = picks.astype(BF16).T.reshape(CHIPS, 16, 128)
        return 0

    lax.fori_loop(0, CHIPS, group, 0, unroll=4)


def table_of(got_ref, table_ref, o):
    pieces = []
    for i in range(4):
        pieces += [got_ref[o, 96 + 16 * i : 112 + 16 * i, :], table_ref[o, 16 * i : 16 * (i + 1), :]]
    return jnp.concatenate(pieces, axis=0)


def add_kernel(near_ref, far_ref, out_ref):
    for j in range(CHIPS):
        out_ref[j] = (near_ref[j].astype(F32) + far_ref[j].astype(F32)).astype(BF16)


def value_kernel(mix_ref, token_ref, got_ref, table_ref, near_ref, far_ref, sums_ref):
    def shard(o, _):
        sums_ref[o] = contract(mix_ref[o], table_of(got_ref, table_ref, o), 1, 0).astype(BF16)
        return 0

    lax.fori_loop(0, CHIPS, shard, 0, unroll=8)
    token_rows = iota((256, GROUP_SLOTS), 0).astype(F32).astype(BF16)

    def group(g, _):
        sums = sums_ref[:, pl.ds(pl.multiple_of(g * 16, 16), 16), :].reshape(GROUP_SLOTS, 128)
        place = token_ref[g, 0:1, :].astype(BF16)
        hits = jnp.where(place == token_rows, jnp.ones((), BF16), jnp.zeros((), BF16))
        out = contract(hits, sums, 1, 0).astype(BF16)
        near_ref[g] = out[:128]
        far_ref[g] = out[128:]
        return 0

    lax.fori_loop(0, CHIPS, group, 0, unroll=8)


def gather_kernel(near_any, far_any, token_ref, rows_ref, near_ref, far_ref, sems):
    chunk = CHIPS // 4
    copies = []
    for i in range(4):
        part = pl.ds(i * chunk, chunk)
        for j, (source, ref) in enumerate(((near_any, near_ref), (far_any, far_ref))):
            copies.append(pltpu.make_async_copy(source.at[part], ref.at[part], sems.at[2 * i + j]))
    for copy in copies:
        copy.start()
    token_rows = iota((256, GROUP_SLOTS), 0).astype(F32).astype(BF16)

    def gather(g, _):
        place = token_ref[g, 0:1, :].astype(BF16)
        hits = jnp.where(place == token_rows, jnp.ones((), BF16), jnp.zeros((), BF16))
        grads = jnp.concatenate([near_ref[g], far_ref[g]], axis=0)
        rows = contract(hits, grads, 0, 0).astype(BF16)
        rows_ref[:, pl.ds(pl.multiple_of(g * 16, 16), 16), :] = rows.reshape(CHIPS, 16, 128)
        return 0

    for i in range(4):
        copies[2 * i].wait()
        copies[2 * i + 1].wait()
        lax.fori_loop(i * chunk, (i + 1) * chunk, gather, 0, unroll=8)


def table_grad_kernel(mix_ref, rows_ref, keep_ref, send_ref):
    def shard(o, _):
        grad = contract(mix_ref[o], rows_ref[o], 0, 0).astype(BF16)
        for m in range(8):
            (send_ref if m & 1 else keep_ref)[m >> 1, o] = grad[16 * m : 16 * (m + 1)]
        return 0

    lax.fori_loop(0, CHIPS, shard, 0, unroll=8)


def fold_kernel(keep_ref, got_ref, *out_refs):
    for i, out_ref in enumerate(out_refs):
        for j in range(CHIPS):
            out_ref[j] = (keep_ref[i, j].astype(F32) + got_ref[i, j].astype(F32)).astype(BF16)


def weight_grad_kernel(rows_ref, pick_ref, token_ref, got_ref, table_ref, near_ref, far_ref, found_ref):
    def shard(o, _):
        scores = contract(rows_ref[o], table_of(got_ref, table_ref, o), 1, 1)
        picks = pick_ref[o].astype(F32).astype(jnp.int32)
        found = jnp.take_along_axis(scores, jnp.maximum(picks, 0), axis=1, mode="promise_in_bounds")
        found_ref[o] = jnp.where(picks >= 0, found, 0.0).astype(BF16)
        return 0

    lax.fori_loop(0, CHIPS, shard, 0, unroll=8)
    fold_rows = iota((64, GROUP_SLOTS), 0).astype(F32).astype(BF16)

    def group(g, _):
        found = found_ref[:, pl.ds(pl.multiple_of(g * 16, 16), 16), :].reshape(GROUP_SLOTS, 128)
        place = token_ref[g, 1:2, :].astype(BF16)
        hits = jnp.where(place == fold_rows, jnp.ones((), BF16), jnp.zeros((), BF16))
        out = contract(hits, found, 1, 0).astype(BF16)
        near_ref[g] = out[:32]
        far_ref[g] = out[32:]
        return 0

    lax.fori_loop(0, CHIPS, group, 0, unroll=8)


def last_kernel(near_ref, far_ref, *refs):
    out_ref = refs[-1]
    for j in range(CHIPS):
        out_ref[j, 0:32, :] = (near_ref[j].astype(F32) + far_ref[j].astype(F32)).astype(BF16)
        total = refs[0][j].astype(F32)
        for ref in refs[1:-1]:
            total += ref[j].astype(F32)
        out_ref[j, 32:48, :] = total.astype(BF16)


def finish_kernel(got_ref, weight_ref, table_ref):
    def add(j, total):
        return total + got_ref[j, 0:32, :].astype(F32)

    total = lax.fori_loop(0, CHIPS, add, jnp.zeros((32, 128), F32), unroll=8)
    total = jnp.concatenate([total[:, 32 * i : 32 * (i + 1)] for i in range(4)], axis=0)
    weight_ref[...] = total.T.astype(BF16)
    for j in range(CHIPS):
        table_ref[:, 128 * j : 128 * (j + 1)] = got_ref[j, 32:48, :]


def call(kernel, out_shapes, *operands, us=1, scratch=(), limit=16, spaces=()):
    vmem = pl.BlockSpec(memory_space=pltpu.VMEM)
    outs = tuple(s if isinstance(s, jax.ShapeDtypeStruct) else jax.ShapeDtypeStruct(s, BF16) for s in out_shapes)
    return pl.pallas_call(
        kernel,
        out_shape=outs,
        in_specs=[pl.BlockSpec(memory_space=s) for s in spaces] + [vmem] * (len(operands) - len(spaces)),
        out_specs=tuple(vmem for _ in outs),
        scratch_shapes=scratch,
        compiler_params=pltpu.CompilerParams(vmem_limit_bytes=limit * 2**20),
        cost_estimate=pl.CostEstimate(
            flops=int(us * 1e9), bytes_accessed=int(us * 3.3e6), transcendentals=0
        ),
    )(*operands)


def swap_cores(v):
    return lax.ppermute(v, "core", [(0, 1), (1, 0)])


def across(v, bits):
    return lax.ppermute(v, "y", [(i, i ^ bits) for i in range(8)])


def exchange(v):
    return lax.all_to_all(v, ("x", "z"), split_axis=0, concat_axis=0, tiled=True)


def after(v, *others):
    return lax.optimization_barrier((v, *others))[0]


def on_device(key_blocks, key_rows, weights, value_table, cotangent):
    own, other = call(
        tag_kernel,
        [(3, 32, 128)] * 2,
        key_blocks.T,
        key_rows.T,
        weights.T,
        us=2,
        scratch=[
            pltpu.VMEM((2, 128), jnp.int32),
            pltpu.VMEM((32, 128), jnp.int32),
            pltpu.VMEM((32, 128), F32),
            pltpu.SemaphoreType.DMA((3,)),
        ],
        limit=60,
        spaces=[pl.ANY] * 3,
    )
    half, grads = call(
        body_kernel,
        [(CHIPS, 64, 128), (CHIPS, 128, 128)],
        after(cotangent, own),
        value_table,
        us=2,
        scratch=[
            pltpu.VMEM((128, 4096), BF16),
            pltpu.VMEM((128, 4096), BF16),
            pltpu.SemaphoreType.DMA((2,)),
        ],
        limit=60,
        spaces=[pl.ANY] * 2,
    )
    other, half, grads = lax.optimization_barrier((swap_cores(other), half, grads))
    (first,) = call(first_kernel, [(CHIPS, 160, 128)], own, other, half, us=0.4)
    got = exchange(first)
    near_grads = exchange(after(grads, got))

    table = across(got[:, 96:, :], 1)
    mix, picks, tokens = call(
        mix_kernel,
        [(CHIPS, GROUP_SLOTS, 128)] * 2 + [jax.ShapeDtypeStruct((CHIPS, 8, GROUP_SLOTS), F32)],
        got,
        us=8.5,
        scratch=[
            pltpu.VMEM((CHIPS * 32, TAGS), BF16),
            pltpu.VMEM((CHIPS * 32, 2 * GROUP_SLOTS), F32),
        ],
    )
    near, far = call(
        value_kernel,
        [(CHIPS, 128, 128)] * 2,
        mix,
        tokens,
        got,
        table,
        us=4.5,
        scratch=[pltpu.VMEM((CHIPS, GROUP_SLOTS, 128), BF16)],
    )
    (out,) = call(add_kernel, [(CHIPS, 128, 128)], near, swap_cores(far), us=0.3)
    got_out = exchange(after(out, near_grads))

    (rows,) = call(
        gather_kernel,
        [(CHIPS, GROUP_SLOTS, 128)],
        near_grads,
        swap_cores(near_grads),
        tokens,
        us=3,
        scratch=[
            pltpu.VMEM((CHIPS, 128, 128), BF16),
            pltpu.VMEM((CHIPS, 128, 128), BF16),
            pltpu.SemaphoreType.DMA((8,)),
        ],
        spaces=[pl.ANY] * 2,
    )
    keep, send = call(table_grad_kernel, [(4, CHIPS, 16, 128)] * 2, mix, rows, us=2.5)
    near, far = call(
        weight_grad_kernel,
        [(CHIPS, 32, 128)] * 2,
        rows,
        picks,
        tokens,
        got,
        table,
        us=8,
        scratch=[pltpu.VMEM((CHIPS, GROUP_SLOTS, 128), BF16)],
    )
    halves = call(fold_kernel, [(CHIPS, 16, 128)] * 4, keep, across(send, 1), us=0.3)
    parts = [halves[0]] + [across(halves[i], 2 * i) for i in (2, 1, 3)]
    (last,) = call(last_kernel, [(CHIPS, 48, 128)], near, swap_cores(far), *parts, us=0.8)
    got_last = exchange(after(last, got_out))
    memory_out = jnp.transpose(got_out, (1, 0, 2)).reshape(128, 4096)
    weight_out, table_out = call(finish_kernel, [(32, 128), (16, 4096)], got_last)
    return memory_out, weight_out.T, table_out


def solution(mesh):
    fine = Mesh(mesh.devices.reshape(4, 8, 2, 8), ("x", "z", "core", "y"))
    tokens = P(("x", "z", "core", "y"), None)
    return jax.shard_map(
        on_device,
        mesh=fine,
        in_specs=(tokens, tokens, tokens, P(("x", "z", "core"), None), tokens),
        out_specs=(tokens, tokens, tokens),
        check_vma=False,
    )
```

```python
import jax
import jax.numpy as jnp
from jax import lax
from jax.experimental import pallas as pl
from jax.experimental.pallas import tpu as pltpu
from jax.sharding import Mesh
from jax.sharding import PartitionSpec as P

CAP = 5
CHIPS = 32
GROUP_SLOTS = 512
TAGS = 384
BF16 = jnp.bfloat16
F32 = jnp.float32


def iota(shape, dim):
    return lax.broadcasted_iota(jnp.int32, shape, dim)


def contract(a, b, da, db):
    return lax.dot_general(a, b, (((da,), (db,)), ((), ())), preferred_element_type=F32)


def prepare_kernel(
    blocks_any,
    rows_any,
    weights_any,
    table_any,
    grads_any,
    own_ref,
    other_ref,
    half_ref,
    out_ref,
    blocks_ref,
    rows_ref,
    weights_ref,
    table_ref,
    grads_ref,
    sems,
):
    anys = (blocks_any, rows_any, weights_any, grads_any, table_any)
    refs = (blocks_ref, rows_ref, weights_ref, grads_ref, table_ref)
    copies = [pltpu.make_async_copy(a, r, sems.at[i]) for i, (a, r) in enumerate(zip(anys, refs))]
    for copy in copies:
        copy.start()
    for copy in copies[:3]:
        copy.wait()
    tags(blocks_ref, rows_ref, weights_ref, own_ref, other_ref)
    copies[3].wait()
    for j in range(CHIPS):
        out_ref[j] = grads_ref[:, 128 * j : 128 * (j + 1)]
    copies[4].wait()
    y = lax.axis_index("y")
    for i in range(4):
        block = (((y >> 1) ^ i) << 1) | (y & 1)
        rows = pl.ds(pl.multiple_of(block * 16, 16), 16)
        for j in range(CHIPS):
            half_ref[j, 16 * i : 16 * (i + 1), :] = table_ref[rows, 128 * j : 128 * (j + 1)]


def tags(blocks_ref, rows_ref, weights_ref, own_ref, other_ref):
    core = lax.axis_index("core")
    n = 256
    owner = jnp.concatenate([blocks_ref[0:1, :], blocks_ref[1:2, :]], axis=1)
    hot = (owner == iota((64, n), 0)).astype(F32)
    upper = (iota((n, n), 0) < iota((n, n), 1)).astype(BF16)
    before = contract(hot.astype(BF16), upper, 1, 0)
    rank = jnp.sum(before * hot, axis=0, keepdims=True).astype(jnp.int32)
    half = owner & 1
    chip = owner >> 1
    rows = rows_ref[...].astype(F32).astype(BF16)
    rows = jnp.concatenate([rows[:16], rows[16:]], axis=1)
    weights = weights_ref[...].astype(BF16)
    weights = jnp.concatenate([weights[:16], weights[16:]], axis=1)
    entry = iota((CHIPS, n), 1) + 1
    lanes = iota((TAGS, n), 0)
    token_place = (lanes == 2 * CHIPS * CAP + core * CAP + rank).astype(F32).astype(BF16)
    for out, mine in ((own_ref, core), (other_ref, 1 - core)):
        slot = jnp.where(half == mine, core * (CHIPS * CAP) + chip * CAP + rank, -1)
        hits = (lanes == slot).astype(F32).astype(BF16)
        tokens = jnp.where(jnp.where(half == mine, chip, -1) == iota((CHIPS, n), 0), entry, 0)
        tokens = tokens.astype(F32).astype(BF16)
        out_tags = jnp.concatenate([contract(rows, hits, 1, 1), contract(weights, hits, 1, 1)], axis=0)
        out_tags = (out_tags + contract(tokens, token_place, 1, 1)).astype(BF16)
        for i in range(3):
            out[i] = out_tags[:, 128 * i : 128 * (i + 1)]


def first_kernel(own_ref, other_ref, half_ref, out_ref):
    tags = own_ref[...].reshape(96, 128) + other_ref[...].reshape(96, 128)
    for j in range(CHIPS):
        out_ref[j, 0:96, :] = tags
        out_ref[j, 96:160, :] = half_ref[j]


def widen(got_ref, tags_ref, wide_ref):
    for g in range(CHIPS):
        for i in range(3):
            tags_ref[g * 32 : (g + 1) * 32, 128 * i : 128 * (i + 1)] = got_ref[g, 32 * i : 32 * (i + 1), :]
    slot = iota((1, GROUP_SLOTS), 1)
    sender, rank = (slot >> 3) & 1, slot & 7
    used = rank < CAP
    lane = jnp.where(used, sender * (CHIPS * CAP) + (slot >> 4) * CAP + rank, -1)
    spread = (iota((TAGS, GROUP_SLOTS), 0) == lane).astype(F32).astype(BF16)
    lane = jnp.where(used, 2 * CHIPS * CAP - 256 + sender * CAP + rank, -1)
    spread_tokens = (iota((128, GROUP_SLOTS), 0) == lane).astype(F32).astype(BF16)
    for i in range(4):
        rows = slice(256 * i, 256 * (i + 1))
        wide_ref[rows, 0:GROUP_SLOTS] = contract(tags_ref[rows, :], spread, 1, 0)
        wide_ref[rows, GROUP_SLOTS : 2 * GROUP_SLOTS] = contract(
            tags_ref[rows, 256:384], spread_tokens, 1, 0
        )


def token_tags(wide_ref, g, shard_of):
    tokens = wide_ref[pl.ds(pl.multiple_of(g * 32, 32), 32), GROUP_SLOTS : 2 * GROUP_SLOTS]
    tag = jnp.sum(jnp.where(shard_of, tokens, 0.0), axis=0, keepdims=True)
    valid = tag > 0.5
    second_block = (tag > 128.5).astype(F32)
    return valid, tag - 1.0 - 128.0 * second_block, second_block


def slot_rows(wide_ref, g):
    rows = wide_ref[pl.ds(pl.multiple_of(g * 32, 32), 16), 0:GROUP_SLOTS]
    return (rows.astype(jnp.int32) ^ (lax.axis_index("y") * 16)).astype(F32)


def slot_masks():
    core = lax.axis_index("core")
    shard_of = iota((CHIPS, GROUP_SLOTS), 1) // 16 == iota((CHIPS, GROUP_SLOTS), 0)
    second = (iota((1, GROUP_SLOTS), 1) & 8) != 0
    return shard_of, jnp.where(second, 1 - core, core).astype(F32)


def mix_kernel(got_ref, mix_ref, pick_ref, token_ref, tags_ref, wide_ref):
    widen(got_ref, tags_ref, wide_ref)
    shard_of, far = slot_masks()
    position = iota((128, GROUP_SLOTS), 0).astype(F32).astype(BF16)

    def group(g, _):
        valid, token, second_block = token_tags(wide_ref, g, shard_of)
        quarter = (
            (token > 31.5).astype(F32) + (token > 63.5).astype(F32) + (token > 95.5).astype(F32)
        )
        token_ref[g, 0:1, :] = jnp.where(valid, far * 128.0 + token, -1.0)
        token_ref[g, 1:2, :] = jnp.where(valid, far * 32.0 + token - 32.0 * quarter, -1.0)
        part = jnp.where(valid, quarter * 2.0 + second_block, -1.0)
        rows = slot_rows(wide_ref, g)
        picks = jnp.concatenate([jnp.where(part == float(i), rows, -1.0) for i in range(8)], axis=0)
        rows = rows.astype(BF16)
        at = pl.multiple_of(g * 32 + 16, 16)
        weights = wide_ref[pl.ds(at, 16), 0:GROUP_SLOTS].astype(BF16)
        mix = jnp.zeros((128, GROUP_SLOTS), BF16)
        for k in range(16):
            mix = jnp.where(rows[k : k + 1, :] == position, weights[k : k + 1, :], mix)
        here = pl.ds(pl.multiple_of(g * 16, 16), 16)
        mix_ref[:, here, :] = mix.T.reshape(CHIPS, 16, 128)
        pick_ref[:, here, :] = picks.astype(BF16).T.reshape(CHIPS, 16, 128)
        return 0

    lax.fori_loop(0, CHIPS, group, 0, unroll=4)


def table_of(got_ref, table_ref, o):
    pieces = []
    for i in range(4):
        pieces += [got_ref[o, 96 + 16 * i : 112 + 16 * i, :], table_ref[o, 16 * i : 16 * (i + 1), :]]
    return jnp.concatenate(pieces, axis=0)


def add_kernel(near_ref, far_ref, out_ref):
    for j in range(CHIPS):
        out_ref[j] = (near_ref[j].astype(F32) + far_ref[j].astype(F32)).astype(BF16)


def value_kernel(mix_ref, token_ref, got_ref, table_ref, near_ref, far_ref, sums_ref):
    def shard(o, _):
        sums_ref[o] = contract(mix_ref[o], table_of(got_ref, table_ref, o), 1, 0).astype(BF16)
        return 0

    lax.fori_loop(0, CHIPS, shard, 0, unroll=8)
    token_rows = iota((256, GROUP_SLOTS), 0).astype(F32).astype(BF16)

    def group(g, _):
        sums = sums_ref[:, pl.ds(pl.multiple_of(g * 16, 16), 16), :].reshape(GROUP_SLOTS, 128)
        place = token_ref[g, 0:1, :].astype(BF16)
        hits = jnp.where(place == token_rows, jnp.ones((), BF16), jnp.zeros((), BF16))
        out = contract(hits, sums, 1, 0).astype(BF16)
        near_ref[g] = out[:128]
        far_ref[g] = out[128:]
        return 0

    lax.fori_loop(0, CHIPS, group, 0, unroll=8)


def gather_kernel(token_ref, near_ref, far_ref, rows_ref):
    token_rows = iota((256, GROUP_SLOTS), 0).astype(F32).astype(BF16)

    def gather(g, _):
        place = token_ref[g, 0:1, :].astype(BF16)
        hits = jnp.where(place == token_rows, jnp.ones((), BF16), jnp.zeros((), BF16))
        grads = jnp.concatenate([near_ref[g], far_ref[g]], axis=0)
        rows = contract(hits, grads, 0, 0).astype(BF16)
        rows_ref[:, pl.ds(pl.multiple_of(g * 16, 16), 16), :] = rows.reshape(CHIPS, 16, 128)
        return 0

    lax.fori_loop(0, CHIPS, gather, 0, unroll=8)


def table_grad_kernel(mix_ref, rows_ref, keep_ref, send_ref):
    def shard(o, _):
        grad = contract(mix_ref[o], rows_ref[o], 0, 0).astype(BF16)
        for m in range(8):
            (send_ref if m & 1 else keep_ref)[m >> 1, o] = grad[16 * m : 16 * (m + 1)]
        return 0

    lax.fori_loop(0, CHIPS, shard, 0, unroll=8)


def fold_kernel(keep_ref, got_ref, *out_refs):
    for i, out_ref in enumerate(out_refs):
        for j in range(CHIPS):
            out_ref[j] = (keep_ref[i, j].astype(F32) + got_ref[i, j].astype(F32)).astype(BF16)


def weight_grad_kernel(rows_ref, pick_ref, token_ref, got_ref, table_ref, near_ref, far_ref, found_ref):
    def shard(o, _):
        scores = contract(rows_ref[o], table_of(got_ref, table_ref, o), 1, 1)
        picks = pick_ref[o].astype(F32).astype(jnp.int32)
        found = jnp.take_along_axis(scores, jnp.maximum(picks, 0), axis=1, mode="promise_in_bounds")
        found_ref[o] = jnp.where(picks >= 0, found, 0.0).astype(BF16)
        return 0

    lax.fori_loop(0, CHIPS, shard, 0, unroll=8)
    fold_rows = iota((64, GROUP_SLOTS), 0).astype(F32).astype(BF16)

    def group(g, _):
        found = found_ref[:, pl.ds(pl.multiple_of(g * 16, 16), 16), :].reshape(GROUP_SLOTS, 128)
        place = token_ref[g, 1:2, :].astype(BF16)
        hits = jnp.where(place == fold_rows, jnp.ones((), BF16), jnp.zeros((), BF16))
        out = contract(hits, found, 1, 0).astype(BF16)
        near_ref[g] = out[:32]
        far_ref[g] = out[32:]
        return 0

    lax.fori_loop(0, CHIPS, group, 0, unroll=8)


def last_kernel(near_ref, far_ref, *refs):
    out_ref = refs[-1]
    for j in range(CHIPS):
        out_ref[j, 0:32, :] = (near_ref[j].astype(F32) + far_ref[j].astype(F32)).astype(BF16)
        total = refs[0][j].astype(F32)
        for ref in refs[1:-1]:
            total += ref[j].astype(F32)
        out_ref[j, 32:48, :] = total.astype(BF16)


def finish_kernel(got_ref, weight_ref, table_ref):
    def add(j, total):
        return total + got_ref[j, 0:32, :].astype(F32)

    total = lax.fori_loop(0, CHIPS, add, jnp.zeros((32, 128), F32), unroll=8)
    total = jnp.concatenate([total[:, 32 * i : 32 * (i + 1)] for i in range(4)], axis=0)
    weight_ref[...] = total.T.astype(BF16)
    for j in range(CHIPS):
        table_ref[:, 128 * j : 128 * (j + 1)] = got_ref[j, 32:48, :]


def call(kernel, out_shapes, *operands, us=1, scratch=(), limit=16, spaces=()):
    vmem = pl.BlockSpec(memory_space=pltpu.VMEM)
    outs = tuple(s if isinstance(s, jax.ShapeDtypeStruct) else jax.ShapeDtypeStruct(s, BF16) for s in out_shapes)
    return pl.pallas_call(
        kernel,
        out_shape=outs,
        in_specs=[pl.BlockSpec(memory_space=s) for s in spaces] + [vmem] * (len(operands) - len(spaces)),
        out_specs=tuple(vmem for _ in outs),
        scratch_shapes=scratch,
        compiler_params=pltpu.CompilerParams(vmem_limit_bytes=limit * 2**20),
        cost_estimate=pl.CostEstimate(
            flops=int(us * 1e9), bytes_accessed=int(us * 3.3e6), transcendentals=0
        ),
    )(*operands)


def swap_cores(v):
    return lax.ppermute(v, "core", [(0, 1), (1, 0)])


def across(v, bits):
    return lax.ppermute(v, "y", [(i, i ^ bits) for i in range(8)])


def exchange(v):
    return lax.all_to_all(v, ("x", "z"), split_axis=0, concat_axis=0, tiled=True)


def after(v, *others):
    return lax.optimization_barrier((v, *others))[0]


def on_device(key_blocks, key_rows, weights, value_table, cotangent):
    own, other, half, grads = call(
        prepare_kernel,
        [(3, 32, 128)] * 2 + [(CHIPS, 64, 128), (CHIPS, 128, 128)],
        key_blocks.T,
        key_rows.T,
        weights.T,
        value_table,
        cotangent,
        us=2,
        scratch=[
            pltpu.VMEM((2, 128), jnp.int32),
            pltpu.VMEM((32, 128), jnp.int32),
            pltpu.VMEM((32, 128), F32),
            pltpu.VMEM((128, 4096), BF16),
            pltpu.VMEM((128, 4096), BF16),
            pltpu.SemaphoreType.DMA((5,)),
        ],
        limit=60,
        spaces=[pl.ANY] * 5,
    )
    other = swap_cores(other)
    (first,) = call(first_kernel, [(CHIPS, 160, 128)], own, other, half, us=0.4)
    got = exchange(first)
    near_grads = exchange(after(grads, got))

    table = across(got[:, 96:, :], 1)
    mix, picks, tokens = call(
        mix_kernel,
        [(CHIPS, GROUP_SLOTS, 128)] * 2 + [jax.ShapeDtypeStruct((CHIPS, 8, GROUP_SLOTS), F32)],
        got,
        us=8.5,
        scratch=[
            pltpu.VMEM((CHIPS * 32, TAGS), BF16),
            pltpu.VMEM((CHIPS * 32, 2 * GROUP_SLOTS), F32),
        ],
    )
    near, far = call(
        value_kernel,
        [(CHIPS, 128, 128)] * 2,
        mix,
        tokens,
        got,
        table,
        us=4.5,
        scratch=[pltpu.VMEM((CHIPS, GROUP_SLOTS, 128), BF16)],
    )
    (out,) = call(add_kernel, [(CHIPS, 128, 128)], near, swap_cores(far), us=0.3)
    got_out = exchange(after(out, near_grads))

    (rows,) = call(
        gather_kernel,
        [(CHIPS, GROUP_SLOTS, 128)],
        tokens,
        near_grads,
        swap_cores(near_grads),
        us=3,
    )
    keep, send = call(table_grad_kernel, [(4, CHIPS, 16, 128)] * 2, mix, rows, us=2.5)
    near, far = call(
        weight_grad_kernel,
        [(CHIPS, 32, 128)] * 2,
        rows,
        picks,
        tokens,
        got,
        table,
        us=8,
        scratch=[pltpu.VMEM((CHIPS, GROUP_SLOTS, 128), BF16)],
    )
    halves = call(fold_kernel, [(CHIPS, 16, 128)] * 4, keep, across(send, 1), us=0.3)
    parts = [halves[0]] + [across(halves[i], 2 * i) for i in (1, 3, 2)]
    (last,) = call(last_kernel, [(CHIPS, 48, 128)], near, swap_cores(far), *parts, us=0.8)
    got_last = exchange(after(last, got_out))
    memory_out = jnp.transpose(got_out, (1, 0, 2)).reshape(128, 4096)
    weight_out, table_out = call(finish_kernel, [(32, 128), (16, 4096)], got_last)
    return memory_out, weight_out.T, table_out


def solution(mesh):
    fine = Mesh(mesh.devices.reshape(4, 8, 2, 8), ("x", "z", "core", "y"))
    tokens = P(("x", "z", "core", "y"), None)
    return jax.shard_map(
        on_device,
        mesh=fine,
        in_specs=(tokens, tokens, tokens, P(("x", "z", "core"), None), tokens),
        out_specs=(tokens, tokens, tokens),
        check_vma=False,
    )
```
